32 devices in a mesh: fsdp: 16 (over z, y, core), heads: 2 (over x).
Axes of the slice: x: 2, y: 2, z: 4, core: 2. Of those that a mesh axis runs over, the one named last changes fastest.
Arguments:
- tokens: bfloat16 [16384, 1024], P(('fsdp', 'heads')), may hold values from -6 to 6
- ln1_gain: bfloat16 [1024], P('fsdp'), may hold values from 0.5 to 1.5
- ln1_bias: bfloat16 [1024], P('fsdp'), may hold values from -3 to 3
- w_query: bfloat16 [1024, 1024], P('fsdp', 'heads'), may hold values from -0.1875 to 0.1875
- w_key: bfloat16 [1024, 1024], P('fsdp', 'heads'), may hold values from -0.1875 to 0.1875
- w_value: bfloat16 [1024, 1024], P('fsdp', 'heads'), may hold values from -0.1875 to 0.1875
- bias_query: bfloat16 [16, 64], P('heads', 'fsdp'), may hold values from -3 to 3
- bias_value: bfloat16 [16, 64], P('heads', 'fsdp'), may hold values from -3 to 3
- w_out: bfloat16 [1024, 1024], P('heads', 'fsdp'), may hold values from -1.5 to 1.5
- bias_out: bfloat16 [1024], P('fsdp'), may hold values from -3 to 3
- ln2_gain: bfloat16 [1024], P('fsdp'), may hold values from 0.5 to 1.5
- ln2_bias: bfloat16 [1024], P('fsdp'), may hold values from -3 to 3
- w_up: bfloat16 [1024, 4096], P('fsdp', 'heads'), may hold values from -0.1875 to 0.1875
- bias_up: bfloat16 [16, 256], P('heads', 'fsdp'), may hold values from -3 to 3
- w_down: bfloat16 [4096, 1024], P('heads', 'fsdp'), may hold values from -0.09375 to 0.09375
- bias_down: bfloat16 [1024], P('fsdp'), may hold values from -3 to 3
- cotangent: bfloat16 [16384, 1024], P(('fsdp', 'heads')), may hold values from -6 to 6
- seq_lengths: int32 [16, 8], P('fsdp'), may hold values from 0 to 1024, as said below
Outputs:
- output: bfloat16 [16384, 1024], P(('fsdp', 'heads'))
- grad_input: float32 [16384, 1024], P(('fsdp', 'heads'))
- grad_ln1_gain: float32 [1024], P(('fsdp', 'heads'))
- grad_ln1_bias: float32 [1024], P(('fsdp', 'heads'))
- grad_w_query: float32 [1024, 1024], P('fsdp', 'heads')
- grad_w_key: float32 [1024, 1024], P('fsdp', 'heads')
- grad_w_value: float32 [1024, 1024], P('fsdp', 'heads')
- grad_bias_query: float32 [16, 64], P('heads', 'fsdp')
- grad_bias_value: float32 [16, 64], P('heads', 'fsdp')
- grad_w_out: float32 [1024, 1024], P('heads', 'fsdp')
- grad_bias_out: float32 [1024], P(('fsdp', 'heads'))
- grad_ln2_gain: float32 [1024], P(('fsdp', 'heads'))
- grad_ln2_bias: float32 [1024], P(('fsdp', 'heads'))
- grad_w_up: float32 [1024, 4096], P('fsdp', 'heads')
- grad_bias_up: float32 [16, 256], P('heads', 'fsdp')
- grad_w_down: float32 [4096, 1024], P('heads', 'fsdp')
- grad_bias_down: float32 [1024], P(('fsdp', 'heads'))
The draws below stay inside these ranges and needn't reach their ends.
Inputs may be any that keep to these rules, and one draw needn't show every extreme that they name: `seq_lengths`: row f lists in order the lengths of the sequences on fsdp group f; a zero marks an empty slot. Each row sums to 512 or more and to 1024 at most, and some row holds one sequence of 1024 tokens.
All inputs are finite; a program needn't handle non-finite values.
Results may differ from the reference program's by a relative error of at most 0.02.
Values may be sent and summed in bfloat16 or wider, within the bound.
No kernel may reach another device: no remote copies, remote signals or barrier semaphores. Data moves between devices by JAX's collectives and lax.ppermute only.
A program may use at most 256 MiB of HBM per device.

```python
import jax
import jax.numpy as jnp
from jax import lax

D = 1024
H = 16
HD = 64
FF = 4096
TOK_DEV = 1024
SLOTS = 8
TOKENS = 16384
N_FSDP = 16


def draw_seq_lengths(key, part):
    key = jax.random.fold_in(key, 7)
    key_total, key_full, key_cuts = jax.random.split(key, 3)
    totals = jax.random.randint(key_total, (N_FSDP,), TOK_DEV // 2, TOK_DEV + 1)
    full_group = jax.random.randint(key_full, (), 0, N_FSDP)
    cuts = jax.random.randint(key_cuts, (N_FSDP, SLOTS - 1), 0, TOK_DEV + 1)
    cuts = jnp.sort(jnp.minimum(cuts, totals[:, None]), axis=1)
    edges = jnp.concatenate([jnp.zeros((N_FSDP, 1), jnp.int32), cuts.astype(jnp.int32), totals[:, None].astype(jnp.int32)], axis=1)
    lengths = edges[:, 1:] - edges[:, :-1]
    single = jnp.zeros((SLOTS,), jnp.int32).at[0].set(TOK_DEV)
    groups = jnp.arange(N_FSDP, dtype=jnp.int32)
    rows = jnp.where((groups == full_group)[:, None], single[None, :], lengths)
    return rows.astype(jnp.int32)


def block_scale(own_key, extent, cuts, smallest, largest):
    loudness = 1.0
    for dim, shards_of in cuts:
        draws = jax.random.uniform(jax.random.fold_in(jax.random.fold_in(own_key, 6), dim), (shards_of,), jnp.float32, smallest / len(cuts), largest / len(cuts))
        loudness = loudness * jnp.repeat(jnp.exp(draws), extent[dim] // shards_of).reshape((-1,) + (1,) * (len(extent) - 1 - dim))
    return loudness


def gaussian(key, extent, deviation, limit, shards=(), held_as=jnp.bfloat16):
    drawn = jax.random.normal(key, extent, jnp.float32) * deviation
    if len(shards) > 0:
        drawn = block_scale(key, extent, shards, -0.22, 0.18) * drawn
    return jnp.clip(drawn, min=-limit, max=limit).astype(held_as)


def setup_inputs(seed: int = 0) -> dict:
    streams_of = jax.random.split(jax.random.key(seed), 19)
    tokens = gaussian(streams_of[0], (TOKENS, D), 1.0, 6.0, ((0, 32),))
    ln1_gain = jnp.clip(1.0 + 0.1 * jax.random.normal(streams_of[1], (D,), jnp.float32), 0.5, 1.5).astype(jnp.bfloat16)
    ln1_bias = gaussian(streams_of[2], (D,), 0.5, 3.0, ((0, 16),))
    w_query = gaussian(streams_of[3], (D, D), D ** -0.5, 0.1875, ((0, 16), (1, 2)))
    w_key = gaussian(streams_of[4], (D, D), D ** -0.5, 0.1875, ((0, 16), (1, 2)))
    w_value = gaussian(streams_of[5], (D, D), D ** -0.5, 0.1875, ((0, 16), (1, 2)))
    bias_query = gaussian(streams_of[6], (H, HD), 0.5, 3.0, ((0, 2), (1, 16)))
    bias_value = gaussian(streams_of[7], (H, HD), 0.5, 3.0, ((0, 2), (1, 16)))
    w_out = gaussian(streams_of[8], (D, D), 16 ** -0.5, 1.5, ((0, 2), (1, 16)))
    bias_out = gaussian(streams_of[9], (D,), 0.5, 3.0, ((0, 16),))
    ln2_gain = jnp.clip(1.0 + 0.1 * jax.random.normal(streams_of[10], (D,), jnp.float32), 0.5, 1.5).astype(jnp.bfloat16)
    ln2_bias = gaussian(streams_of[11], (D,), 0.5, 3.0, ((0, 16),))
    w_up = gaussian(streams_of[12], (D, FF), D ** -0.5, 0.1875, ((0, 16), (1, 2)))
    bias_up = gaussian(streams_of[13], (H, FF // H), 0.5, 3.0, ((0, 2), (1, 16)))
    w_down = gaussian(streams_of[14], (FF, D), FF ** -0.5, 0.09375, ((0, 2), (1, 16)))
    bias_down = gaussian(streams_of[15], (D,), 0.5, 3.0, ((0, 16),))
    cotangent = gaussian(streams_of[16], (TOKENS, D), 1.0, 6.0, ((0, 32),))
    seq_lengths = draw_seq_lengths(jax.random.fold_in(streams_of[18], 71), 0)
    return dict(tokens=tokens, ln1_gain=ln1_gain, ln1_bias=ln1_bias, w_query=w_query, w_key=w_key, w_value=w_value, bias_query=bias_query, bias_value=bias_value, w_out=w_out, bias_out=bias_out, ln2_gain=ln2_gain, ln2_bias=ln2_bias, w_up=w_up, bias_up=bias_up, w_down=w_down, bias_down=bias_down, cotangent=cotangent, seq_lengths=seq_lengths)


@jax.custom_vjp
def low(v):
    return lax.optimization_barrier(v.astype(jnp.bfloat16)).astype(jnp.float32)

@jax.custom_vjp
def low_back(v):
    return v

def low_keep(v):
    return (low(v), None)

def low_pass(kept, grad):
    return (grad,)

def back_keep(v):
    return (v, None)

def back_low(kept, grad):
    return (low(grad),)
low.defvjp(low_keep, low_pass)
low_back.defvjp(back_keep, back_low)
EPSILON = 1e-05
GELU_SCALE = 0.7978845608028654
MASKED = -1e+30
BEST = lax.Precision.HIGHEST

def norm_rows(rows, gain, shift):
    mean = lax.optimization_barrier(jnp.mean(rows, axis=-1, keepdims=True))
    centered = rows - mean
    var = lax.optimization_barrier(jnp.mean(centered * centered, axis=-1, keepdims=True))
    return centered * lax.rsqrt(var + EPSILON) * gain + shift

def gelu(pre):
    return 0.5 * pre * (1.0 + jnp.tanh(GELU_SCALE * (pre + 0.044715 * pre * pre * pre)))

def matmul(left, right):
    return jnp.dot(left, right, precision=BEST)

def group_layer(params, rows, lengths):
    gain_one, shift_one, query_w, key_w, value_w, query_b, value_b, out_w, out_b, gain_two, shift_two, up_w, up_b, down_w, down_b = params
    ends = jnp.cumsum(lengths).astype(jnp.int32)
    positions = jnp.arange(TOK_DEV, dtype=jnp.int32)
    segment = lax.optimization_barrier(jnp.sum((ends[None, :] <= positions[:, None]).astype(jnp.int32), axis=1))
    allowed = (segment[:, None] == segment[None, :]) & (positions[None, :] <= positions[:, None])
    normed_one = low(norm_rows(rows, gain_one, shift_one))
    query = low(low_back(matmul(normed_one, query_w) + query_b.reshape(-1)))
    key = low(low_back(matmul(normed_one, key_w)))
    value = low(low_back(matmul(normed_one, value_w) + value_b.reshape(-1)))
    query = query.reshape(TOK_DEV, H, HD)
    key = key.reshape(TOK_DEV, H, HD)
    value = value.reshape(TOK_DEV, H, HD)
    scores = jnp.einsum('qhd,khd->hqk', query, key, precision=BEST) * HD ** (-0.5)
    scores = low_back(jnp.where(allowed[None], scores, MASKED))
    top = lax.optimization_barrier(jnp.max(scores, axis=-1, keepdims=True))
    weights = jnp.exp(scores - top)
    probs = weights / lax.optimization_barrier(jnp.sum(weights, axis=-1, keepdims=True))
    mixed = jnp.einsum('hqk,khd->qhd', low(probs), value, precision=BEST).reshape(TOK_DEV, D)
    mixed = low(low_back(mixed))
    mid = rows + low_back(matmul(mixed, out_w) + out_b)
    normed_two = low(norm_rows(mid, gain_two, shift_two))
    hidden = low(gelu(low_back(matmul(normed_two, up_w) + up_b.reshape(-1))))
    return mid + matmul(hidden, down_w) + down_b

def reference(tokens, ln1_gain, ln1_bias, w_query, w_key, w_value, bias_query, bias_value, w_out, bias_out, ln2_gain, ln2_bias, w_up, bias_up, w_down, bias_down, cotangent, seq_lengths):
    params = tuple((p.astype(jnp.float32) for p in (ln1_gain, ln1_bias, w_query, w_key, w_value, bias_query, bias_value, w_out, bias_out, ln2_gain, ln2_bias, w_up, bias_up, w_down, bias_down)))
    rows_all = tokens.astype(jnp.float32).reshape(N_FSDP, TOK_DEV, D)
    ends_all = jnp.cumsum(seq_lengths, axis=1).astype(jnp.int32)
    positions = jnp.arange(TOK_DEV, dtype=jnp.int32)
    live = (positions[None, :] < ends_all[:, -1:]).astype(jnp.float32)
    grad_rows = cotangent.astype(jnp.float32).reshape(N_FSDP, TOK_DEV, D) * live[:, :, None]

    def forward(weights, rows):

        def step(carry, item):
            return (carry, jax.checkpoint(group_layer)(weights, item[0], item[1]))
        _, result = lax.scan(step, jnp.zeros((), jnp.float32), (rows, seq_lengths))
        return result
    result, pull = jax.vjp(forward, params, rows_all)
    grad_params, grad_rows_in = pull(grad_rows)
    g_gain_one, g_shift_one, g_query_w, g_key_w, g_value_w, g_query_b, g_value_b, g_out_w, g_out_b, g_gain_two, g_shift_two, g_up_w, g_up_b, g_down_w, g_down_b = grad_params
    return (result.reshape(TOKENS, D).astype(jnp.bfloat16), grad_rows_in.reshape(TOKENS, D), g_gain_one, g_shift_one, g_query_w, g_key_w, g_value_w, g_query_b, g_value_b, g_out_w, g_out_b, g_gain_two, g_shift_two, g_up_w, g_up_b, g_down_w, g_down_b)
```

```python
import functools

import jax
import jax.numpy as jnp
from jax import lax
from jax.experimental import pallas as pl
from jax.experimental.pallas import tpu as pltpu
from jax.sharding import PartitionSpec as P

HD = 64
PAIR = 2 * HD
EPSILON = 1e-05
GELU_SCALE = 0.7978845608028654
MASKED = -1e30
F32 = jnp.float32
BF = jnp.bfloat16
NN = (((1,), (0,)), ((), ()))
NT = (((1,), (1,)), ((), ()))
TN = (((0,), (0,)), ((), ()))


def dot(left, right, dims=NN):
    return lax.dot_general(left, right, dims, preferred_element_type=F32)


def starts_of(ends_ref, position):
    start = jnp.zeros_like(position)
    for slot in range(ends_ref.shape[0]):
        start = jnp.where(position >= ends_ref[slot], ends_ref[slot], start)
    return start


def place(block, step, shift, rows):
    return pl.ds(pl.multiple_of(lax.rem(block * step + shift, rows), step), step)


def attend_kernel(rows, step, shift_ref, ends_ref, qkv_ref, mixed_ref, turned_ref, log_ref, keys, values, bias):
    shift = shift_ref[0]

    @pl.when(pl.program_id(0) == 0)
    def _():
        for i in range(rows // step):
            wide = (i + 1) * step
            row = lax.broadcasted_iota(jnp.int32, (step, 1), 0) + i * step
            column = lax.broadcasted_iota(jnp.int32, (step, wide), 1)
            seen = (column >= starts_of(ends_ref, row)) & (column <= row)
            bias[i * step : wide, :wide] = jnp.where(seen, 0.0, MASKED)

    for b in range(rows // step):
        keys[b * step : (b + 1) * step, :] = qkv_ref[place(b, step, shift, rows), PAIR : 2 * PAIR]
        values[b * step : (b + 1) * step, :] = qkv_ref[place(b, step, shift, rows), 2 * PAIR :]
    lane = lax.broadcasted_iota(jnp.int32, (step, PAIR), 1)
    second = lane >= HD
    for i in range(rows // step):
        wide = (i + 1) * step
        query = qkv_ref[place(i, step, shift, rows), :PAIR] * jnp.asarray(HD**-0.5, BF)
        mixed, logs = [], []
        for h in range(2):
            own = jnp.where(second == (h == 1), query, jnp.zeros_like(query))
            scores = dot(own, keys[:wide, :], NT) + bias[i * step : wide, :wide]
            top = jnp.max(scores, axis=1, keepdims=True)
            weights = jnp.exp(scores - top)
            total = jnp.sum(weights, axis=1, keepdims=True)
            mixed.append(dot(weights.astype(BF), values[:wide, :]) * (1.0 / total))
            logs.append(top + jnp.log(total))
        mixed = jnp.where(second, mixed[1], mixed[0]).astype(BF)
        mixed_ref[place(i, step, shift, rows), :] = mixed
        turned_ref[place(i, step, shift + rows // 2, rows), :] = mixed
        log_ref[0, :, i * step : wide] = jnp.transpose(jnp.where(lane >= 4, logs[1], logs[0]))[:8]


def attend_back_kernel(
    rows, step, shift_ref, ends_ref, qkv_ref, grad_ref, log_ref, out_ref, keys, values, bias, key_sum, value_sum
):
    shift = shift_ref[0]

    @pl.when(pl.program_id(0) == 0)
    def _():
        for i in range(rows // step):
            wide = (i + 1) * step
            row = lax.broadcasted_iota(jnp.int32, (1, step), 1) + i * step
            column = lax.broadcasted_iota(jnp.int32, (wide, step), 0)
            seen = (column >= starts_of(ends_ref, row)) & (column <= row)
            bias[:wide, i * step : wide] = jnp.where(seen, 0.0, MASKED)

    for b in range(rows // step):
        keys[b * step : (b + 1) * step, :] = qkv_ref[place(b, step, shift, rows), PAIR : 2 * PAIR]
        values[b * step : (b + 1) * step, :] = qkv_ref[place(b, step, shift, rows), 2 * PAIR :]
    second = lax.broadcasted_iota(jnp.int32, (step, PAIR), 1) >= HD
    for i in reversed(range(rows // step)):
        low, wide = i * step, (i + 1) * step
        query = qkv_ref[place(i, step, shift, rows), :PAIR] * jnp.asarray(HD**-0.5, BF)
        grad = grad_ref[place(i, step, shift, rows), :]
        to_query, to_key, to_value = [], [], []
        for h in range(2):
            own_query = jnp.where(second == (h == 1), query, jnp.zeros_like(query))
            own_grad = jnp.where(second == (h == 1), grad, jnp.zeros_like(grad))
            scores = dot(keys[:wide, :], own_query, NT) + bias[:wide, low:wide]
            probs = jnp.exp(scores - log_ref[0, 4 * h : 4 * h + 1, low:wide])
            grad_probs = dot(values[:wide, :], own_grad, NT)
            spread = jnp.sum(probs * grad_probs, axis=0, keepdims=True)
            grad_scores = (probs * (grad_probs - spread)).astype(BF)
            to_value.append(dot(probs.astype(BF), own_grad))
            to_key.append(dot(grad_scores, own_query))
            to_query.append(dot(grad_scores, keys[:wide, :], TN))
        grad_query = jnp.where(second, to_query[1], to_query[0]) * (HD**-0.5)
        grad_key = to_key[0] + to_key[1]
        grad_value = to_value[0] + to_value[1]
        if wide < rows:
            grad_key = grad_key + key_sum[:wide, :]
            grad_value = grad_value + value_sum[:wide, :]
        out_ref[place(i, step, shift, rows), :PAIR] = grad_query.astype(BF)
        out_ref[place(i, step, shift, rows), PAIR : 2 * PAIR] = grad_key[low:, :].astype(BF)
        out_ref[place(i, step, shift, rows), 2 * PAIR :] = grad_value[low:, :].astype(BF)
        if low > 0:
            key_sum[:low, :] = grad_key[:low, :]
            value_sum[:low, :] = grad_value[:low, :]


def attend(shift, ends, qkv, pairs):
    rows = qkv.shape[0]
    step = min(256, rows)
    work = 2 * pairs * rows * rows
    return pl.pallas_call(
        functools.partial(attend_kernel, rows, step),
        grid_spec=pltpu.PrefetchScalarGridSpec(
            num_scalar_prefetch=2,
            grid=(pairs,),
            in_specs=[pl.BlockSpec((rows, 3 * PAIR), lambda p, *_: (0, p))],
            out_specs=[
                pl.BlockSpec((rows, PAIR), lambda p, *_: (0, p)),
                pl.BlockSpec((rows, PAIR), lambda p, *_: (0, p)),
                pl.BlockSpec((1, 8, rows), lambda p, *_: (p, 0, 0)),
            ],
            scratch_shapes=[
                pltpu.VMEM((rows, PAIR), BF),
                pltpu.VMEM((rows, PAIR), BF),
                pltpu.VMEM((rows, rows), F32),
            ],
        ),
        out_shape=[
            jax.ShapeDtypeStruct((rows, PAIR * pairs), BF),
            jax.ShapeDtypeStruct((rows, PAIR * pairs), BF),
            jax.ShapeDtypeStruct((pairs, 8, rows), F32),
        ],
        compiler_params=pltpu.CompilerParams(vmem_limit_bytes=40 << 20),
        cost_estimate=pl.CostEstimate(
            flops=work * 512, bytes_accessed=rows * PAIR * pairs * 8, transcendentals=work // 2
        ),
        name="attend",
    )(shift, ends, qkv)


def attend_back(shift, ends, qkv, grad_mixed, logs, first, pairs):
    rows = qkv.shape[0]
    step = min(256, rows)
    work = 2 * pairs * rows * rows
    return pl.pallas_call(
        functools.partial(attend_back_kernel, rows, step),
        grid_spec=pltpu.PrefetchScalarGridSpec(
            num_scalar_prefetch=2,
            grid=(pairs,),
            in_specs=[
                pl.BlockSpec((rows, 3 * PAIR), lambda p, *_: (0, p)),
                pl.BlockSpec((rows, PAIR), lambda p, *_: (0, p + first)),
                pl.BlockSpec((1, 8, rows), lambda p, *_: (p, 0, 0)),
            ],
            out_specs=pl.BlockSpec((rows, 3 * PAIR), lambda p, *_: (0, p)),
            scratch_shapes=[
                pltpu.VMEM((rows, PAIR), BF),
                pltpu.VMEM((rows, PAIR), BF),
                pltpu.VMEM((rows, rows), F32),
                pltpu.VMEM((rows, PAIR), F32),
                pltpu.VMEM((rows, PAIR), F32),
            ],
        ),
        out_shape=jax.ShapeDtypeStruct((rows, 3 * PAIR * pairs), BF),
        compiler_params=pltpu.CompilerParams(vmem_limit_bytes=40 << 20),
        cost_estimate=pl.CostEstimate(
            flops=work * 1280, bytes_accessed=rows * PAIR * pairs * 14, transcendentals=work // 2
        ),
        name="attend_back",
    )(shift, ends, qkv, grad_mixed, logs)


BITS = 4


def lined():
    return lax.axis_size("fsdp") == 1 << BITS


def bit_of(axis):
    return (lax.axis_index("fsdp") >> (BITS - 1 - axis)) & 1


def trade(array, axis):
    flip = 1 << (BITS - 1 - axis)
    return lax.ppermute(array, "fsdp", [(i, i ^ flip) for i in range(1 << BITS)])


def after(array, *earlier):
    earlier = tuple(e for e in earlier if e is not None)
    return lax.optimization_barrier((array,) + earlier)[0] if earlier else array


def interleave_kernel(core_ref, own_ref, other_ref, out_ref):
    core = core_ref[0]
    out_ref[0, core] = own_ref[0]
    out_ref[0, 1 - core] = other_ref[0]


def interleave(core, own, other):
    n, r, c = own.shape
    spec = pl.BlockSpec((1, r, c), lambda i, *_: (i, 0, 0))
    return pl.pallas_call(
        interleave_kernel,
        grid_spec=pltpu.PrefetchScalarGridSpec(
            num_scalar_prefetch=1,
            grid=(n,),
            in_specs=[spec, spec],
            out_specs=pl.BlockSpec((1, 2, r, c), lambda i, *_: (i, 0, 0, 0)),
        ),
        out_shape=jax.ShapeDtypeStruct((n, 2, r, c), own.dtype),
        compiler_params=pltpu.CompilerParams(vmem_limit_bytes=32 << 20),
        cost_estimate=pl.CostEstimate(flops=0, bytes_accessed=own.size * 8, transcendentals=0),
        name="interleave",
    )(core.reshape(1).astype(jnp.int32), own, other)


class Gather:
    def __init__(self, shard, order=(0, 1, 2)):
        self.block, self.order, self.passed, self.width = shard, list(order), [], shard.shape[1]

    def step(self, *earlier):
        if not lined():
            if not self.passed:
                self.block = lax.all_gather(after(self.block, *earlier), "fsdp", axis=0, tiled=True)
                self.passed = [0]
            return self.block
        axis = self.order.pop(0)
        at = sum(p < axis for p in self.passed)
        self.passed.append(axis)
        block = after(self.block, *earlier)
        other = trade(block, axis)
        self.block = jnp.where(bit_of(axis) == 1, jnp.stack([other, block], at), jnp.stack([block, other], at))
        return other

    def end(self, *earlier):
        if not lined():
            self.step(*earlier)
            return self.block
        while self.order:
            self.step(*earlier)
        block = after(self.block, *earlier).reshape(8, -1, self.width)
        other = trade(block, 3)
        if block.shape[1] * self.width < 1 << 15:
            whole = jnp.where(bit_of(3) == 1, jnp.stack([other, block], 1), jnp.stack([block, other], 1))
        else:
            whole = interleave(bit_of(3), block, other)
        return whole.reshape(-1, self.width)


def at_index(array, index, axis):
    return lax.dynamic_index_in_dim(array, index, axis, keepdims=False)


def halve(parts, axis):
    own = bit_of(axis)
    got = trade(at_index(parts, 1 - own, axis), axis)
    return (at_index(parts, own, axis).astype(F32) + got.astype(F32)).astype(parts.dtype)


class Vectors:
    def __init__(self, whole):
        self.axes = [3, 2, 1, 0] if lined() else []
        if lined():
            self.parts = whole.reshape((2,) * BITS + (whole.shape[0] >> BITS, whole.shape[1]))
        else:
            self.parts = lax.psum_scatter(whole, "fsdp", scatter_dimension=0, tiled=True)

    def step(self, *earlier):
        if not self.axes:
            return None
        self.parts = halve(after(self.parts, *earlier), self.axes.pop(0))
        return self.parts


def columns_of(array, index):
    width = array.shape[1] // 2
    return lax.dynamic_slice_in_dim(array, index * width, width, 1)


class Weigh:
    def __init__(self, left, right, order=(2, 1, 0)):
        self.order = list(order)
        if not lined():
            self.order = []
            self.parts = lax.psum_scatter(dot(left, right, TN).astype(BF), "fsdp", scatter_dimension=0, tiled=True)
            return
        core = bit_of(3)
        got = trade(dot(left, columns_of(right, 1 - core), TN).astype(BF), 3)
        total = (dot(left, columns_of(right, core), TN) + got.astype(F32)).astype(BF)
        self.parts = total.reshape(2, 2, 2, -1, total.shape[1])
        self.left = [0, 1, 2]

    def step(self, *earlier):
        if not self.order:
            return None
        axis = self.order.pop(0)
        at = self.left.index(axis)
        self.left.remove(axis)
        parts = after(self.parts, *earlier)
        own = bit_of(axis)
        got = trade(at_index(parts, 1 - own, at), axis)
        total = at_index(parts, own, at).astype(F32) + got.astype(F32)
        self.parts = total if not self.order else total.astype(BF)
        return got

    def end(self, *earlier):
        if not lined():
            return self.parts.astype(F32)
        total = after(self.parts, *earlier)
        core = bit_of(3)
        total = total.reshape(2, -1, total.shape[1])
        got = trade(at_index(total, 1 - core, 0).astype(BF), 3).astype(F32)
        own = at_index(total, core, 0)
        return jnp.where(core == 1, jnp.concatenate([got, own], 1), jnp.concatenate([own, got], 1))


def paired():
    return lax.axis_size("heads") == 2


def swap(array):
    return lax.ppermute(array, "heads", [(0, 1), (1, 0)])


def heads_rows(share):
    if not paired():
        return lax.all_gather(share, "heads", axis=0, tiled=True)
    return jnp.concatenate([share, swap(share)], 0)


def heads_columns(share):
    if not paired():
        return lax.all_gather(share, "heads", axis=1, tiled=True)
    return jnp.concatenate([share, swap(share)], 1)


def heads_partials(left, right, dims):
    if not paired():
        return [dot(left, right, dims)]
    share = left.shape[0] // 2
    theirs = dot(left[share:], right, dims)
    return [dot(left[:share], right, dims), theirs]


def heads_sum(partials, *earlier):
    if not paired():
        return lax.psum_scatter(partials[0].astype(BF), "heads", scatter_dimension=0, tiled=True).astype(F32)
    return partials[0].astype(F32) + swap(after(partials[1].astype(BF), *earlier)).astype(F32)


def heads_exchange(columns):
    if not paired():
        return lax.all_to_all(columns, "heads", 1, 0, tiled=True)
    width = columns.shape[1] // 2
    return jnp.concatenate([columns[:, :width], swap(columns[:, width:])], 0)


def norm_parts(rows):
    mean = jnp.mean(rows, axis=-1, keepdims=True)
    centered = rows - mean
    scale = lax.rsqrt(jnp.mean(centered * centered, axis=-1, keepdims=True) + EPSILON)
    return centered * scale, scale


def norm_back(grad, hat, scale, gain):
    e = grad * gain
    return scale * (e - jnp.mean(e, -1, keepdims=True) - hat * jnp.mean(e * hat, -1, keepdims=True))


def local(
    tokens,
    ln1_gain,
    ln1_bias,
    w_query,
    w_key,
    w_value,
    bias_query,
    bias_value,
    w_out,
    bias_out,
    ln2_gain,
    ln2_bias,
    w_up,
    bias_up,
    w_down,
    bias_down,
    cotangent,
    seq_lengths,
):
    share = tokens.shape[0]
    rows = share * lax.axis_size("heads")
    depth = ln1_gain.shape[0]
    width = w_query.shape[1]
    pairs = width // PAIR
    groups = [(0, pairs)] if pairs < 2 else [(0, pairs // 2), (pairs // 2, pairs - pairs // 2)]
    here = lax.axis_index("heads")
    shift = (here * share if paired() else jnp.zeros((), jnp.int32)).astype(jnp.int32).reshape(1)
    ends = jnp.cumsum(seq_lengths[0]).astype(jnp.int32)
    live = (here * share + jnp.arange(share, dtype=jnp.int32) < ends[-1]).astype(F32)

    shards = []
    for first, count in groups:
        columns = [w[:, p * PAIR : (p + 1) * PAIR] for p in range(first, first + count) for w in (w_query, w_key, w_value)]
        shards.append(Gather(jnp.concatenate(columns, 1)))
    tokens_other = swap(tokens) if paired() else None
    kinds = [ln1_gain, ln1_bias, bias_out, ln2_gain, ln2_bias, bias_down]
    shorts = [bias_up, bias_query, bias_value]
    lines = [v.reshape(1, depth) for v in kinds]
    short = jnp.concatenate([v.reshape(-1) for v in shorts])
    lines.append(jnp.pad(short, (0, -short.shape[0] % depth)).reshape(-1, depth))
    lines = jnp.concatenate(lines, 0)
    lines = jnp.pad(lines, ((0, -lines.shape[0] % 16), (0, 128 - depth)))
    small = Gather(lines)
    out_shard = Gather(heads_columns(w_out.T))
    up_shard = Gather(w_up)
    down_shard = Gather(w_down.T, (2, 0, 1))
    full_width = out_shard.width
    if lined() and len(shards) == 2:
        ended = [shards[0].step(), small.step()]
        ended = [shards[0].step(*ended), small.step(*ended), shards[1].step(*ended)]
        ended = [shards[0].step(*ended), small.step(*ended), shards[1].step(*ended), out_shard.step(*ended)]
        qkv_w = [shards[0].end(*ended)]
        flat = small.end(*ended)
        pending = [shards[1].step(*ended), out_shard.step(*ended), up_shard.step(*ended)]
    else:
        qkv_w = [shards[0].end()]
        flat = small.end()
        pending = []
    flat = flat.reshape(lax.axis_size("fsdp"), -1, 128)[:, :, :depth].astype(F32)
    vectors = jnp.swapaxes(flat[:, :6], 0, 1).reshape(6, 1, -1)
    gain_one, shift_one, out_b, gain_two, shift_two, down_b = [vectors[i] for i in range(6)]
    short = flat[:, 6:].reshape(flat.shape[0], -1)
    at = 0
    tail = []
    for shard in shorts:
        part = short[:, at : at + shard.size].reshape((-1,) + shard.shape)
        tail.append(jnp.swapaxes(part, 0, 1).reshape(1, -1))
        at += shard.size
    up_b, query_b, value_b = tail
    qkv_b = jnp.stack([query_b.reshape(pairs, PAIR), jnp.zeros((pairs, PAIR), F32), value_b.reshape(pairs, PAIR)], 1)
    qkv_b = qkv_b.reshape(1, -1)

    grad_out = (cotangent.astype(F32) * live[:, None]).astype(BF)
    if paired():
        rows_full = jnp.concatenate([tokens, tokens_other], 0).astype(F32)
    else:
        rows_full = lax.all_gather(tokens, "heads", axis=0, tiled=True).astype(F32)
    own_rows = lambda array: lax.dynamic_slice_in_dim(array, 0 if paired() else here * share, share, 0)
    hat_one, scale_one = norm_parts(rows_full)
    normed_one = (hat_one * gain_one + shift_one).astype(BF)
    mixed, others, logs, qkv = [], [], [], []
    for g, (first, count) in enumerate(groups):
        if g > 0:
            pending = [p for p in pending if p is not None]
            qkv_w.append(shards[g].end(mixed[-1], *pending))
            if lined():
                pending = [out_shard.step(mixed[-1], *pending), down_shard.step(mixed[-1]), up_shard.step(mixed[-1], *pending)]
        bias = qkv_b[:, first * 3 * PAIR : (first + count) * 3 * PAIR]
        qkv.append((dot(normed_one, qkv_w[-1]) + bias).astype(BF))
        part, turned, log = attend(shift, ends, qkv[-1], count)
        mixed.append(part)
        logs.append(log)
        if paired():
            others.append(swap(after(turned, others[-1] if others else tokens_other)))
    out_w = out_shard.end(mixed[-1])
    if lined():
        pending = [up_shard.step(mixed[-1], *pending), down_shard.step(mixed[-1], *pending)]
    up_w = up_shard.end(*pending[:1])
    down_w = down_shard.end(*pending)
    mixed = jnp.concatenate(mixed, 1)
    if paired():
        mixed_full = jnp.concatenate([mixed] + others, 1)
    else:
        mixed_full = lax.all_gather(mixed, "heads", axis=1, tiled=True)
    grad_out_full = heads_rows(after(grad_out, mixed_full))
    mid = rows_full + dot(mixed_full, out_w, NT) + out_b
    hat_two, scale_two = norm_parts(mid)
    normed_two = (hat_two * gain_two + shift_two).astype(BF)
    pre = dot(normed_two, up_w) + up_b
    squared = pre * pre
    bend = jnp.tanh(GELU_SCALE * (pre + 0.044715 * pre * squared))
    hidden = (0.5 * pre * (1.0 + bend)).astype(BF)
    slope = 0.5 * (1.0 + bend) + 0.5 * pre * (1.0 - bend * bend) * GELU_SCALE * (1.0 + 3 * 0.044715 * squared)

    grad_pre = (slope * dot(grad_out_full, down_w)).astype(BF)
    partials_two = heads_partials(grad_pre, up_w, NT)
    down_sum = Weigh(grad_out_full, hidden)
    up_sum = Weigh(normed_two, grad_pre, (1, 0, 2))
    grad_normed_two = heads_sum(partials_two)
    grad_mid = grad_out.astype(F32) + norm_back(
        after(grad_normed_two, down_sum.parts, up_sum.parts), own_rows(hat_two), own_rows(scale_two), gain_two
    )
    grad_branch = grad_mid.astype(BF)
    mixing = heads_exchange(dot(grad_branch, out_w).astype(BF))
    out_sum = Weigh(grad_branch, own_rows(mixed_full))
    partials = lax.optimization_barrier(heads_partials(hidden, down_w, NT))
    hats = jnp.split(hat_two, len(partials_two))
    grad_gain_two = sum(jnp.sum(p * h, 0) for p, h in zip(partials_two, hats))
    grad_shift_two = sum(jnp.sum(p, 0) for p in partials_two)
    grad_up_b = jnp.sum(grad_pre, axis=0, dtype=F32)

    grad_mixed = after(mixing, out_sum.parts, grad_gain_two, grad_shift_two, grad_up_b)
    ended = [down_sum.step(), up_sum.step()]
    feedforward = heads_sum(partials, mixing)
    grad_qkv, sums = [], []
    for g, ((first, count), log, part) in enumerate(zip(groups, logs, qkv)):
        if g > 0:
            sums.append(Weigh(normed_one, grad_qkv[-1]))
            grad_mixed = after(grad_mixed, grad_qkv[-1], sums[-1].parts, down_sum.parts, up_sum.parts)
            ended = [down_sum.step(grad_qkv[-1]), up_sum.step(grad_qkv[-1]), out_sum.step(grad_qkv[-1])]
        part = attend_back(shift, ends, part, grad_mixed, log, first, count)
        grad_qkv.append(part)
    partials_one = heads_partials(jnp.concatenate(grad_qkv, 1), jnp.concatenate(qkv_w, 1), NT)
    partials_one = lax.optimization_barrier(partials_one)
    grad_normed_one = heads_sum(partials_one, feedforward)
    sums.append(Weigh(after(normed_one, partials_one[-1]), grad_qkv[-1]))
    hats = jnp.split(hat_one, len(partials_one))
    grad_gain_one = sum(jnp.sum(p * h, 0) for p, h in zip(partials_one, hats))
    grad_shift_one = sum(jnp.sum(p, 0) for p in partials_one)
    grad_qkv_b = jnp.concatenate([jnp.sum(part, axis=0, dtype=F32) for part in grad_qkv]).reshape(pairs, 3, PAIR)

    blocks = lax.axis_size("fsdp")
    heads = bias_query.shape[0]
    wide = [
        v.reshape(blocks, depth)
        for v in (
            grad_gain_one,
            grad_shift_one,
            jnp.sum(grad_branch, axis=0, dtype=F32),
            grad_gain_two,
            grad_shift_two,
            jnp.sum(grad_out, axis=0, dtype=F32),
        )
    ]
    narrow = [
        jnp.swapaxes(v.reshape(heads, blocks, -1), 0, 1).reshape(blocks, -1)
        for v in (grad_up_b, grad_qkv_b[:, 0], grad_qkv_b[:, 2])
    ]
    packed = jnp.concatenate(wide + narrow, 1)
    used = packed.shape[1]
    padded = -(-used // 1024) * 1024
    packed = jnp.pad(packed, ((0, 0), (0, padded - used))).reshape(blocks * (padded // 128), 128)
    packed = Vectors(packed)
    lines = [sums[0], down_sum, up_sum, out_sum, sums[-1], packed]
    ended = [e for e in ended if e is not None] + [sums[-1].parts]
    for _ in range(4):
        ended = [e for e in [line.step(*ended) for line in lines] if e is not None]
    grad_down_w = down_sum.end(*ended)
    grad_up_w = up_sum.end(*ended)
    grad_out_w = out_sum.end(*ended)
    grad_qkv_w = jnp.concatenate([line.end(*ended) for line in sums], 1).reshape(depth, pairs, 3, PAIR)
    if paired():
        width_out = grad_out_w.shape[1] // 2
        grad_out_w = grad_out_w[:, :width_out] + swap(grad_out_w[:, width_out:])
    else:
        grad_out_w = lax.psum_scatter(grad_out_w, "heads", scatter_dimension=1, tiled=True)
    output = (own_rows(mid) + feedforward + down_b).astype(BF)
    grad_input = grad_mid + norm_back(grad_normed_one, own_rows(hat_one), own_rows(scale_one), gain_one)
    packed = packed.parts.reshape(-1)
    over_heads = packed[: 6 * depth].reshape(6, -1, depth // lax.axis_size("heads"))
    if paired():
        theirs = lax.dynamic_index_in_dim(over_heads, 1 - here, 1, keepdims=False)
        vector = lax.dynamic_index_in_dim(over_heads, here, 1, keepdims=False) + swap(theirs)
    else:
        vector = lax.psum(over_heads, "heads")
        vector = lax.dynamic_index_in_dim(vector, here, 1, keepdims=False)
    at = 6 * depth
    flat_grads = []
    for shard in (bias_up, bias_query, bias_value):
        flat_grads.append(packed[at : at + shard.size].reshape(shard.shape))
        at += shard.size
    return (
        output,
        grad_input,
        vector[0],
        vector[1],
        grad_qkv_w[:, :, 0].reshape(depth, width),
        grad_qkv_w[:, :, 1].reshape(depth, width),
        grad_qkv_w[:, :, 2].reshape(depth, width),
        flat_grads[1],
        flat_grads[2],
        grad_out_w.T,
        vector[2],
        vector[3],
        vector[4],
        grad_up_w,
        flat_grads[0],
        grad_down_w.T,
        vector[5],
    )


def solution(mesh):
    in_specs = (
        P(("fsdp", "heads"), None),
        P("fsdp"),
        P("fsdp"),
        P("fsdp", "heads"),
        P("fsdp", "heads"),
        P("fsdp", "heads"),
        P("heads", "fsdp"),
        P("heads", "fsdp"),
        P("heads", "fsdp"),
        P("fsdp"),
        P("fsdp"),
        P("fsdp"),
        P("fsdp", "heads"),
        P("heads", "fsdp"),
        P("heads", "fsdp"),
        P("fsdp"),
        P(("fsdp", "heads"), None),
        P("fsdp", None),
    )
    out_specs = (
        P(("fsdp", "heads"), None),
        P(("fsdp", "heads"), None),
        P(("fsdp", "heads")),
        P(("fsdp", "heads")),
        P("fsdp", "heads"),
        P("fsdp", "heads"),
        P("fsdp", "heads"),
        P("heads", "fsdp"),
        P("heads", "fsdp"),
        P("heads", "fsdp"),
        P(("fsdp", "heads")),
        P(("fsdp", "heads")),
        P(("fsdp", "heads")),
        P("fsdp", "heads"),
        P("heads", "fsdp"),
        P("heads", "fsdp"),
        P(("fsdp", "heads")),
    )
    return jax.shard_map(local, mesh=mesh, in_specs=in_specs, out_specs=out_specs, check_vma=False)
```

```python
import functools

import jax
import jax.numpy as jnp
from jax import lax
from jax.experimental import pallas as pl
from jax.experimental.pallas import tpu as pltpu
from jax.sharding import PartitionSpec as P

HD = 64
PAIR = 2 * HD
EPSILON = 1e-05
GELU_SCALE = 0.7978845608028654
MASKED = -1e30
F32 = jnp.float32
BF = jnp.bfloat16
NN = (((1,), (0,)), ((), ()))
NT = (((1,), (1,)), ((), ()))
TN = (((0,), (0,)), ((), ()))


def dot(left, right, dims=NN):
    return lax.dot_general(left, right, dims, preferred_element_type=F32)


def starts_of(ends_ref, position):
    start = jnp.zeros_like(position)
    for slot in range(ends_ref.shape[0]):
        start = jnp.where(position >= ends_ref[slot], ends_ref[slot], start)
    return start


def place(block, step, shift, rows):
    return pl.ds(pl.multiple_of(lax.rem(block * step + shift, rows), step), step)


def attend_kernel(rows, step, shift_ref, ends_ref, qkv_ref, mixed_ref, turned_ref, log_ref, keys, values, bias):
    shift = shift_ref[0]

    @pl.when(pl.program_id(0) == 0)
    def _():
        for i in range(rows // step):
            wide = (i + 1) * step
            row = lax.broadcasted_iota(jnp.int32, (step, 1), 0) + i * step
            column = lax.broadcasted_iota(jnp.int32, (step, wide), 1)
            seen = (column >= starts_of(ends_ref, row)) & (column <= row)
            bias[i * step : wide, :wide] = jnp.where(seen, 0.0, MASKED)

    for b in range(rows // step):
        keys[b * step : (b + 1) * step, :] = qkv_ref[place(b, step, shift, rows), PAIR : 2 * PAIR]
        values[b * step : (b + 1) * step, :] = qkv_ref[place(b, step, shift, rows), 2 * PAIR :]
    lane = lax.broadcasted_iota(jnp.int32, (step, PAIR), 1)
    second = lane >= HD
    for i in range(rows // step):
        wide = (i + 1) * step
        query = qkv_ref[place(i, step, shift, rows), :PAIR] * jnp.asarray(HD**-0.5, BF)
        mixed, logs = [], []
        for h in range(2):
            own = jnp.where(second == (h == 1), query, jnp.zeros_like(query))
            scores = dot(own, keys[:wide, :], NT) + bias[i * step : wide, :wide]
            top = jnp.max(scores, axis=1, keepdims=True)
            weights = jnp.exp(scores - top)
            total = jnp.sum(weights, axis=1, keepdims=True)
            mixed.append(dot(weights.astype(BF), values[:wide, :]) * (1.0 / total))
            logs.append(top + jnp.log(total))
        mixed = jnp.where(second, mixed[1], mixed[0]).astype(BF)
        mixed_ref[place(i, step, shift, rows), :] = mixed
        turned_ref[place(i, step, shift + rows // 2, rows), :] = mixed
        log_ref[0, :, i * step : wide] = jnp.transpose(jnp.where(lane >= 4, logs[1], logs[0]))[:8]


def attend_back_kernel(
    rows, step, shift_ref, ends_ref, qkv_ref, grad_ref, log_ref, out_ref, keys, values, bias, key_sum, value_sum
):
    shift = shift_ref[0]

    @pl.when(pl.program_id(0) == 0)
    def _():
        for i in range(rows // step):
            wide = (i + 1) * step
            row = lax.broadcasted_iota(jnp.int32, (1, step), 1) + i * step
            column = lax.broadcasted_iota(jnp.int32, (wide, step), 0)
            seen = (column >= starts_of(ends_ref, row)) & (column <= row)
            bias[:wide, i * step : wide] = jnp.where(seen, 0.0, MASKED)

    for b in range(rows // step):
        keys[b * step : (b + 1) * step, :] = qkv_ref[place(b, step, shift, rows), PAIR : 2 * PAIR]
        values[b * step : (b + 1) * step, :] = qkv_ref[place(b, step, shift, rows), 2 * PAIR :]
    second = lax.broadcasted_iota(jnp.int32, (step, PAIR), 1) >= HD
    for i in reversed(range(rows // step)):
        low, wide = i * step, (i + 1) * step
        query = qkv_ref[place(i, step, shift, rows), :PAIR] * jnp.asarray(HD**-0.5, BF)
        grad = grad_ref[place(i, step, shift, rows), :]
        to_query, to_key, to_value = [], [], []
        for h in range(2):
            own_query = jnp.where(second == (h == 1), query, jnp.zeros_like(query))
            own_grad = jnp.where(second == (h == 1), grad, jnp.zeros_like(grad))
            scores = dot(keys[:wide, :], own_query, NT) + bias[:wide, low:wide]
            probs = jnp.exp(scores - log_ref[0, 4 * h : 4 * h + 1, low:wide])
            grad_probs = dot(values[:wide, :], own_grad, NT)
            spread = jnp.sum(probs * grad_probs, axis=0, keepdims=True)
            grad_scores = (probs * (grad_probs - spread)).astype(BF)
            to_value.append(dot(probs.astype(BF), own_grad))
            to_key.append(dot(grad_scores, own_query))
            to_query.append(dot(grad_scores, keys[:wide, :], TN))
        grad_query = jnp.where(second, to_query[1], to_query[0]) * (HD**-0.5)
        grad_key = to_key[0] + to_key[1]
        grad_value = to_value[0] + to_value[1]
        if wide < rows:
            grad_key = grad_key + key_sum[:wide, :]
            grad_value = grad_value + value_sum[:wide, :]
        out_ref[place(i, step, shift, rows), :PAIR] = grad_query.astype(BF)
        out_ref[place(i, step, shift, rows), PAIR : 2 * PAIR] = grad_key[low:, :].astype(BF)
        out_ref[place(i, step, shift, rows), 2 * PAIR :] = grad_value[low:, :].astype(BF)
        if low > 0:
            key_sum[:low, :] = grad_key[:low, :]
            value_sum[:low, :] = grad_value[:low, :]


def attend(shift, ends, qkv, pairs):
    rows = qkv.shape[0]
    step = min(256, rows)
    work = 2 * pairs * rows * rows
    return pl.pallas_call(
        functools.partial(attend_kernel, rows, step),
        grid_spec=pltpu.PrefetchScalarGridSpec(
            num_scalar_prefetch=2,
            grid=(pairs,),
            in_specs=[pl.BlockSpec((rows, 3 * PAIR), lambda p, *_: (0, p))],
            out_specs=[
                pl.BlockSpec((rows, PAIR), lambda p, *_: (0, p)),
                pl.BlockSpec((rows, PAIR), lambda p, *_: (0, p)),
                pl.BlockSpec((1, 8, rows), lambda p, *_: (p, 0, 0)),
            ],
            scratch_shapes=[
                pltpu.VMEM((rows, PAIR), BF),
                pltpu.VMEM((rows, PAIR), BF),
                pltpu.VMEM((rows, rows), F32),
            ],
        ),
        out_shape=[
            jax.ShapeDtypeStruct((rows, PAIR * pairs), BF),
            jax.ShapeDtypeStruct((rows, PAIR * pairs), BF),
            jax.ShapeDtypeStruct((pairs, 8, rows), F32),
        ],
        compiler_params=pltpu.CompilerParams(vmem_limit_bytes=40 << 20),
        cost_estimate=pl.CostEstimate(
            flops=work * 128, bytes_accessed=rows * PAIR * pairs * 8, transcendentals=0
        ),
        name="attend",
    )(shift, ends, qkv)


def attend_back(shift, ends, qkv, grad_mixed, logs, first, pairs):
    rows = qkv.shape[0]
    step = min(256, rows)
    work = 2 * pairs * rows * rows
    return pl.pallas_call(
        functools.partial(attend_back_kernel, rows, step),
        grid_spec=pltpu.PrefetchScalarGridSpec(
            num_scalar_prefetch=2,
            grid=(pairs,),
            in_specs=[
                pl.BlockSpec((rows, 3 * PAIR), lambda p, *_: (0, p)),
                pl.BlockSpec((rows, PAIR), lambda p, *_: (0, p + first)),
                pl.BlockSpec((1, 8, rows), lambda p, *_: (p, 0, 0)),
            ],
            out_specs=pl.BlockSpec((rows, 3 * PAIR), lambda p, *_: (0, p)),
            scratch_shapes=[
                pltpu.VMEM((rows, PAIR), BF),
                pltpu.VMEM((rows, PAIR), BF),
                pltpu.VMEM((rows, rows), F32),
                pltpu.VMEM((rows, PAIR), F32),
                pltpu.VMEM((rows, PAIR), F32),
            ],
        ),
        out_shape=jax.ShapeDtypeStruct((rows, 3 * PAIR * pairs), BF),
        compiler_params=pltpu.CompilerParams(vmem_limit_bytes=40 << 20),
        cost_estimate=pl.CostEstimate(
            flops=work * 256, bytes_accessed=rows * PAIR * pairs * 14, transcendentals=0
        ),
        name="attend_back",
    )(shift, ends, qkv, grad_mixed, logs)


def norm_kernel(parts, gain_ref, shift_ref, *refs):
    part = pl.program_id(0) // (pl.num_programs(0) // parts)
    for i in range(parts):

        @pl.when(part == i)
        def _(i=i):
            rows = refs[i][...].astype(F32)
            centered = rows - jnp.mean(rows, axis=-1, keepdims=True)
            scale = lax.rsqrt(jnp.mean(centered * centered, axis=-1, keepdims=True) + EPSILON)
            refs[parts][...] = (centered * scale * gain_ref[...] + shift_ref[...]).astype(BF)


def norm_all(arrays, gain, shift):
    share, width = arrays[0].shape
    step = min(256, share)
    per, parts = share // step, len(arrays)
    line = pl.BlockSpec((1, width), lambda i: (0, 0))
    return pl.pallas_call(
        functools.partial(norm_kernel, parts),
        grid=(per * parts,),
        in_specs=[line, line]
        + [
            pl.BlockSpec((step, width), lambda i, k=k: (jnp.clip(i - k * per, 0, per - 1), 0))
            for k in range(parts)
        ],
        out_specs=pl.BlockSpec((step, width), lambda i: (i, 0)),
        out_shape=jax.ShapeDtypeStruct((share * parts, width), BF),
        compiler_params=pltpu.CompilerParams(vmem_limit_bytes=32 << 20),
        cost_estimate=pl.CostEstimate(flops=0, bytes_accessed=share * parts * width * 4, transcendentals=0),
        name="norm_all",
    )(gain, shift, *arrays)


def spread_kernel(depth, units, each, pairs, flat_ref, wide_ref, up_ref, qkv_ref):
    devices = flat_ref.shape[0]

    def laid(row, lane, size):
        total = devices * size
        source = flat_ref[:, row, :]
        at = lax.broadcasted_iota(jnp.int32, (128, total), 1) & (size - 1)
        pick = (lax.broadcasted_iota(jnp.int32, (128, total), 0) == at + lane).astype(BF)
        owner = lax.broadcasted_iota(jnp.int32, (devices, total), 1) // size
        mine = owner == lax.broadcasted_iota(jnp.int32, (devices, total), 0)
        return jnp.sum(jnp.where(mine, dot(source, pick), 0.0), axis=0, keepdims=True)

    for i in range(6):
        wide_ref[i : i + 1, :] = laid(i, 0, depth)
    for h in range(2 * pairs):
        up_ref[:, h * devices * units : (h + 1) * devices * units] = laid(8 + h, 0, units)
    for p in range(pairs):
        for k in range(3):
            column = (3 * p + k) * PAIR
            if k == 1:
                qkv_ref[:, column : column + PAIR] = jnp.zeros((1, PAIR), F32)
                continue
            lane = units + (each if k == 2 else 0)
            halves = [laid(8 + 2 * p + h, lane, each) for h in range(2)]
            qkv_ref[:, column : column + PAIR] = jnp.concatenate(halves, 1)


def spread(flat, depth, units, each, pairs):
    devices = flat.shape[0]
    shapes = [(6, devices * depth), (1, 2 * pairs * devices * units), (1, 3 * PAIR * pairs)]
    return pl.pallas_call(
        functools.partial(spread_kernel, depth, units, each, pairs),
        out_shape=[jax.ShapeDtypeStruct(shape, F32) for shape in shapes],
        compiler_params=pltpu.CompilerParams(vmem_limit_bytes=32 << 20),
        name="spread",
    )(flat)


def feed_kernel(normed_ref, grad_ref, up_ref, down_ref, bias_ref, hidden_ref, out_ref, sum_ref):
    step = min(256, normed_ref.shape[0])
    total = None
    for i in range(normed_ref.shape[0] // step):
        rows = slice(i * step, (i + 1) * step)
        pre = dot(normed_ref[rows, :], up_ref[...]) + bias_ref[...]
        squared = pre * pre
        bend = 0.5 + 0.5 * jnp.tanh(pre * (GELU_SCALE + (GELU_SCALE * 0.044715) * squared))
        hidden = pre * bend
        hidden_ref[rows, :] = hidden.astype(BF)
        slope = bend + hidden * (1.0 - bend) * (2 * GELU_SCALE + (6 * GELU_SCALE * 0.044715) * squared)
        grad = (slope * dot(grad_ref[rows, :], down_ref[...])).astype(BF)
        out_ref[rows, :] = grad
        part = jnp.sum(grad.astype(F32), axis=0, keepdims=True)
        total = part if total is None else total + part
    sum_ref[...] = total


def feed(normed, grad_out, up_w, down_w, up_b):
    rows, width = normed.shape
    units = up_w.shape[1]
    step = min(512, units)
    whole = pl.BlockSpec((rows, width), lambda i: (0, 0))
    columns = pl.BlockSpec((width, step), lambda i: (0, i))
    line = pl.BlockSpec((1, step), lambda i: (0, i))
    out = pl.BlockSpec((rows, step), lambda i: (0, i))
    return pl.pallas_call(
        feed_kernel,
        grid=(units // step,),
        in_specs=[whole, whole, columns, columns, line],
        out_specs=[out, out, line],
        out_shape=[
            jax.ShapeDtypeStruct((rows, units), BF),
            jax.ShapeDtypeStruct((rows, units), BF),
            jax.ShapeDtypeStruct((1, units), F32),
        ],
        compiler_params=pltpu.CompilerParams(vmem_limit_bytes=44 << 20),
        cost_estimate=pl.CostEstimate(flops=rows * units * width, bytes_accessed=1 << 20, transcendentals=0),
        name="feed",
    )(normed, grad_out, up_w, down_w, up_b)


BITS = 4


def lined():
    return lax.axis_size("fsdp") == 1 << BITS


def bit_of(axis):
    return (lax.axis_index("fsdp") >> (BITS - 1 - axis)) & 1


def trade(array, axis):
    flip = 1 << (BITS - 1 - axis)
    return lax.ppermute(array, "fsdp", [(i, i ^ flip) for i in range(1 << BITS)])


def after(array, *earlier):
    earlier = tuple(e for e in earlier if e is not None)
    return lax.optimization_barrier((array,) + earlier)[0] if earlier else array


def interleave_kernel(core_ref, own_ref, other_ref, out_ref):
    core = core_ref[0]
    for i in range(own_ref.shape[0]):
        out_ref[i, core] = own_ref[i]
        out_ref[i, 1 - core] = other_ref[i]


def interleave(core, own, other):
    n, r, c = own.shape
    per = 2
    spec = pl.BlockSpec((per, r, c), lambda i, *_: (i, 0, 0))
    return pl.pallas_call(
        interleave_kernel,
        grid_spec=pltpu.PrefetchScalarGridSpec(
            num_scalar_prefetch=1,
            grid=(n // per,),
            in_specs=[spec, spec],
            out_specs=pl.BlockSpec((per, 2, r, c), lambda i, *_: (i, 0, 0, 0)),
        ),
        out_shape=jax.ShapeDtypeStruct((n, 2, r, c), own.dtype),
        compiler_params=pltpu.CompilerParams(vmem_limit_bytes=32 << 20),
        cost_estimate=pl.CostEstimate(flops=0, bytes_accessed=own.size * 8, transcendentals=0),
        name="interleave",
    )(core.reshape(1).astype(jnp.int32), own, other)


def placed(parts):
    array, other, axis, at = parts
    if other is None:
        return array
    return jnp.where(bit_of(axis) == 1, jnp.stack([other, array], at), jnp.stack([array, other], at))


class Gather:
    def __init__(self, shard, order=(0, 1, 2)):
        self.parts, self.order, self.passed, self.width = (shard, None, 0, 0), list(order), [], shard.shape[1]
        self.payload = None

    def take(self, earlier):
        array, other, axis, at = self.parts
        if other is None:
            return after(array, *earlier)
        array, other = after((array, other), *earlier)
        return placed((array, other, axis, at))

    def step(self, *earlier):
        block = self.take(earlier)
        if not lined():
            if not self.passed:
                block = lax.all_gather(block, "fsdp", axis=0, tiled=True)
                self.parts, self.passed = (block, None, 0, 0), [0]
            return block
        axis = self.order.pop(0)
        at = sum(p < axis for p in self.passed)
        self.passed.append(axis)
        self.payload = block
        other = trade(block, axis)
        self.parts = (block, other, axis, at)
        return other

    def end(self, *earlier):
        if not lined():
            return self.step(*earlier)
        while self.order:
            self.step(*earlier)
        block = self.take(earlier).reshape(8, -1, self.width)
        other = trade(block, 3)
        if block.shape[1] * self.width < 1 << 15:
            whole = placed((block, other, 3, 1))
        else:
            whole = interleave(bit_of(3), block, other)
        return whole.reshape(-1, self.width)


def at_index(array, index, axis):
    return lax.dynamic_index_in_dim(array, index, axis, keepdims=False)


class Halver:
    def __init__(self, parts, axes, order, last):
        self.own, self.got, self.left, self.order, self.last = parts, None, list(axes), list(order), last
        self.payload, self.result = None, None

    def take(self, earlier):
        if self.got is None:
            return after(self.own, *earlier)
        own, got = after((self.own, self.got), *earlier)
        total = own.astype(F32) + got.astype(F32)
        return total if not self.order and self.last else total.astype(own.dtype)

    def step(self, *earlier):
        if not self.order:
            return None
        axis = self.order[0]
        at = self.left.index(axis)
        parts = self.take(earlier)
        self.order.pop(0)
        self.left.remove(axis)
        mine = bit_of(axis)
        self.payload = at_index(parts, 1 - mine, at)
        self.got = trade(self.payload, axis)
        self.own = at_index(parts, mine, at)
        return self.got


class Exchange:
    def __init__(self, whole):
        self.rows, self.got, self.payload, self.result = whole.shape[0], None, None, None
        if lined():
            self.own, self.order = whole.reshape((4, 4, -1) + whole.shape[1:]), [1, 0]
        else:
            self.own, self.order = lax.psum_scatter(whole, "fsdp", scatter_dimension=0, tiled=True), []

    def take(self, earlier):
        own, got = after((self.own, tuple(self.got or ())), *earlier)
        return own + sum(got) if got else own

    def step(self, *earlier):
        parts = self.take(earlier)
        at = self.order.pop(0)
        mine = (lax.axis_index("fsdp") >> (0 if at else 2)) & 3
        self.own = at_index(parts, mine, at)
        self.got = []
        for flip in range(1, 4):
            pairs = [(i, i ^ (flip << (0 if at else 2))) for i in range(16)]
            self.got.append(lax.ppermute(at_index(parts, mine ^ flip, at), "fsdp", pairs))
        return self.got[-1]


def columns_of(array, index):
    width = array.shape[1] // 2
    return lax.dynamic_slice_in_dim(array, index * width, width, 1)


class Weigh(Halver):
    def __init__(self, left, right, order=(2, 1, 0)):
        if not lined():
            total = lax.psum_scatter(dot(left, right, TN).astype(BF), "fsdp", scatter_dimension=0, tiled=True)
            super().__init__(total.astype(F32), (), (), True)
            return
        core = bit_of(3)
        got = trade(dot(left, columns_of(right, 1 - core), TN).astype(BF), 3)
        total = (dot(left, columns_of(right, core), TN) + got.astype(F32)).astype(BF)
        super().__init__(total.reshape(2, 2, 2, -1, total.shape[1]), (0, 1, 2), order, True)

    def end(self, *earlier):
        total = self.take(earlier)
        if not lined():
            return total
        core = bit_of(3)
        total = total.reshape(2, -1, total.shape[1])
        got = trade(at_index(total, 1 - core, 0).astype(BF), 3)
        return at_index(total, core, 0), got


def joined(result):
    if not lined():
        return result
    own, got = result[0], result[1].astype(F32)
    return jnp.where(bit_of(3) == 1, jnp.concatenate([got, own], 1), jnp.concatenate([own, got], 1))


def unpack_kernel(count, core_ref, *refs):
    core = core_ref[0]
    for g in range(count):
        for half, part in enumerate(refs[2 * g : 2 * g + 2]):
            pair = 2 * g + (core if half == 0 else 1 - core)
            columns = pl.ds(pl.multiple_of(pair * PAIR, PAIR), PAIR)
            for k in range(3):
                refs[2 * count + 2 + k][:, columns] = part[:, k * PAIR : (k + 1) * PAIR].astype(F32)
    width = refs[2 * count].shape[1]
    for half in range(2):
        place_at = core if half == 0 else 1 - core
        columns = pl.ds(pl.multiple_of(place_at * width, 128), width)
        refs[2 * count + 5][:, columns] = refs[2 * count + half][...].astype(F32)


def unpack(core, groups, up):
    rows, width = groups[0][0].shape[0], len(groups) * 2 * PAIR
    shapes = [(rows, width)] * 3 + [(rows, 2 * up[0].shape[1])]
    return pl.pallas_call(
        functools.partial(unpack_kernel, len(groups)),
        in_specs=[pl.BlockSpec(memory_space=pltpu.SMEM)]
        + [pl.BlockSpec(memory_space=pltpu.VMEM)] * (2 * len(groups) + 2),
        out_specs=[pl.BlockSpec(memory_space=pltpu.VMEM)] * 4,
        out_shape=[jax.ShapeDtypeStruct(shape, F32) for shape in shapes],
        compiler_params=pltpu.CompilerParams(vmem_limit_bytes=32 << 20),
        name="unpack",
    )(core.reshape(1).astype(jnp.int32), *[half for group in groups for half in group], *up)


def pack_kernel(counts, *refs):
    weights, outs, pair = refs[:3], refs[3:], 0
    for out, count in zip(outs, counts):
        for p in range(count):
            for k in range(3):
                column = (3 * p + k) * PAIR
                out[:, column : column + PAIR] = weights[k][:, pair * PAIR : (pair + 1) * PAIR]
            pair += 1


def pack(weights, counts):
    rows = weights[0].shape[0]
    return pl.pallas_call(
        functools.partial(pack_kernel, counts),
        out_shape=[jax.ShapeDtypeStruct((rows, 3 * PAIR * count), BF) for count in counts],
        compiler_params=pltpu.CompilerParams(vmem_limit_bytes=32 << 20),
        name="pack",
    )(*weights)


def lines_kernel(*refs):
    lines, out, rows = refs[:-2], refs[-2], refs[-1]
    rows[...] = jnp.zeros_like(rows)
    for i, line in enumerate(lines[:6]):
        rows[i : i + 1, : line.shape[1]] = line[...].astype(F32)
    lane = 0
    for line in lines[6:]:
        rows[8 : 8 + line.shape[0], lane : lane + line.shape[1]] = line[...].astype(F32)
        lane += line.shape[1]
    out[...] = rows[...].astype(BF)


def pack_lines(lines):
    return pl.pallas_call(
        lines_kernel,
        out_shape=jax.ShapeDtypeStruct((16, 128), BF),
        scratch_shapes=[pltpu.VMEM((16, 128), F32)],
        compiler_params=pltpu.CompilerParams(vmem_limit_bytes=32 << 20),
        name="pack_lines",
    )(*lines)


def paired():
    return lax.axis_size("heads") == 2


def swap(array):
    return lax.ppermute(array, "heads", [(0, 1), (1, 0)])


def heads_rows(share):
    if not paired():
        return lax.all_gather(share, "heads", axis=0, tiled=True)
    return jnp.concatenate([share, swap(share)], 0)


def heads_columns(share):
    if not paired():
        return lax.all_gather(share, "heads", axis=1, tiled=True)
    return jnp.concatenate([share, swap(share)], 1)


def heads_partials(left, right, dims):
    if not paired():
        return [dot(left, right, dims)]
    share = left.shape[0] // 2
    theirs = dot(left[share:], right, dims)
    return [dot(left[:share], right, dims), theirs]


def heads_send(partials, *earlier):
    if not paired():
        partial = after(partials[0].astype(BF), *earlier)
        return lax.psum_scatter(partial, "heads", scatter_dimension=0, tiled=True)
    return swap(after(partials[1].astype(BF), *earlier))


def heads_sum(partials, got):
    return partials[0].astype(F32) + got.astype(F32) if paired() else got.astype(F32)


def heads_exchange(columns):
    if not paired():
        return lax.all_to_all(columns, "heads", 1, 0, tiled=True)
    width = columns.shape[1] // 2
    return jnp.concatenate([columns[:, :width], swap(columns[:, width:])], 0)


def norm_parts(rows):
    mean = jnp.mean(rows, axis=-1, keepdims=True)
    centered = rows - mean
    scale = lax.rsqrt(jnp.mean(centered * centered, axis=-1, keepdims=True) + EPSILON)
    return centered * scale, scale


def norm_back(grad, hat, scale, gain):
    e = grad * gain
    return scale * (e - jnp.mean(e, -1, keepdims=True) - hat * jnp.mean(e * hat, -1, keepdims=True))


def local(
    tokens,
    ln1_gain,
    ln1_bias,
    w_query,
    w_key,
    w_value,
    bias_query,
    bias_value,
    w_out,
    bias_out,
    ln2_gain,
    ln2_bias,
    w_up,
    bias_up,
    w_down,
    bias_down,
    cotangent,
    seq_lengths,
):
    share = tokens.shape[0]
    rows = share * lax.axis_size("heads")
    depth = ln1_gain.shape[0]
    width = w_query.shape[1]
    pairs = width // PAIR
    groups = [(0, pairs)] if pairs < 2 else [(0, pairs // 2), (pairs // 2, pairs - pairs // 2)]
    here = lax.axis_index("heads")
    shift = (here * share if paired() else jnp.zeros((), jnp.int32)).astype(jnp.int32).reshape(1)
    ends = jnp.cumsum(seq_lengths[0]).astype(jnp.int32)
    live = (here * share + jnp.arange(share, dtype=jnp.int32) < ends[-1]).astype(F32)

    blocks, heads, units, each = lax.axis_size("fsdp"), bias_query.shape[0], bias_up.shape[1], bias_query.shape[1]
    shards = [Gather(a) for a in pack((w_query, w_key, w_value), [count for _, count in groups])]
    vectors = (ln1_gain, ln1_bias, bias_out, ln2_gain, ln2_bias, bias_down)
    lines = [v.reshape(1, depth) for v in after(vectors, shards[0].parts[0])] + [bias_up, bias_query, bias_value]
    small = Gather(pack_lines(lines))
    tokens_other = swap(tokens) if paired() else None
    out_shard = Gather(heads_columns(w_out.T))
    up_shard = Gather(w_up)
    down_shard = Gather(w_down.T)
    full_width = out_shard.width
    rounds = lined() and len(shards) == 2
    if rounds:
        ended = [shards[0].step(), small.step()]
        ended = [shards[0].step(*ended), small.step(*ended), shards[1].step(*ended)]
        ended += [tokens_other]
        ended = [shards[0].step(*ended), small.step(*ended), shards[1].step(*ended), out_shard.step(*ended)]
        qkv_w = [shards[0].end(*ended)]
        flat = small.end(*ended)
        ended = [shards[1].step(*ended), out_shard.step(*ended), up_shard.step(*ended)]
    else:
        qkv_w = [shard.end() for shard in shards]
        flat = small.end()
    vectors, up_b, qkv_b = spread(flat.reshape(blocks, -1, 128), depth, units, each, pairs)
    gain_one, shift_one, out_b, gain_two, shift_two, down_b = [vectors[i : i + 1] for i in range(6)]

    grad_out = (cotangent.astype(F32) * live[:, None]).astype(BF)
    grad_out_full = heads_rows(after(grad_out, tokens_other))
    if paired():
        rows_full = jnp.concatenate([tokens, tokens_other], 0).astype(F32)
    else:
        rows_full = lax.all_gather(tokens, "heads", axis=0, tiled=True).astype(F32)
    own_rows = lambda array: lax.dynamic_slice_in_dim(array, 0 if paired() else here * share, share, 0)
    normed_one = norm_all([tokens, tokens_other] if paired() else [rows_full], gain_one, shift_one)
    mixed, others, logs, qkv = [], [], [], []
    for g, (first, count) in enumerate(groups):
        bias = qkv_b[:, first * 3 * PAIR : (first + count) * 3 * PAIR]
        projected = (dot(normed_one, qkv_w[g]) + bias).astype(BF)
        if rounds and g == 0:
            projected = after(projected, *ended)
            qkv_w.append(shards[1].end(projected))
            out_shard.step(projected)
            up_shard.step(projected)
            down_shard.step(projected)
            projected = after(projected, out_shard.payload, up_shard.payload)
        elif rounds:
            up_shard.step(mixed[0])
            down_shard.step(mixed[0])
            projected = after(projected, up_shard.payload, down_shard.payload)
        qkv.append(projected)
        part, turned, log = attend(shift, ends, projected, count)
        mixed.append(part)
        logs.append(log)
        if paired():
            others.append(swap(after(turned, others[-1] if others else grad_out_full)))
    down_shard.step(mixed[-1])
    out_w = out_shard.end(mixed[-1])
    up_w = up_shard.end(out_w)
    down_w = down_shard.end(out_w)
    mixed = jnp.concatenate(mixed, 1)
    if paired():
        mixed_full = jnp.concatenate([mixed] + others, 1)
    else:
        mixed_full = lax.all_gather(mixed, "heads", axis=1, tiled=True)
    mid = rows_full + dot(mixed_full, out_w, NT) + out_b
    hat_two, scale_two = norm_parts(mid)
    normed_two = (hat_two * gain_two + shift_two).astype(BF)

    hidden, grad_pre, grad_up_b = feed(normed_two, grad_out_full, up_w, down_w, up_b)
    partials_two = heads_partials(grad_pre, up_w, NT)
    got_two = heads_send(partials_two)
    down_sum = Weigh(grad_out_full, hidden)
    up_sum = Weigh(normed_two, grad_pre, (1, 0, 2))
    down_sum.step()
    grad_mid = grad_out.astype(F32) + norm_back(
        heads_sum(partials_two, after(got_two, up_sum.own, down_sum.payload)), own_rows(hat_two), own_rows(scale_two), gain_two
    )
    grad_branch = grad_mid.astype(BF)
    up_sum.step()
    mixing = heads_exchange(dot(after(grad_branch, up_sum.payload), out_w).astype(BF))
    out_sum = Weigh(grad_branch, own_rows(mixed_full))
    partials = lax.optimization_barrier(heads_partials(hidden, down_w, NT))
    hats = jnp.split(hat_two, len(partials_two))
    grad_gain_two = sum(jnp.sum(p * h, 0) for p, h in zip(partials_two, hats))
    grad_shift_two = sum(jnp.sum(p, 0) for p in partials_two)

    out_sum.step()
    grad_mixed = after(mixing, out_sum.own, out_sum.payload, grad_gain_two, grad_shift_two)
    got_forward = heads_send(partials, mixing)
    grad_qkv, sums = [], []
    for g, ((first, count), log, part) in enumerate(zip(groups, logs, qkv)):
        if g > 0:
            sums.append(Weigh(normed_one, grad_qkv[-1]))
            lines = [sums[-1], up_sum, down_sum, out_sum]
            for line in lines:
                line.step(grad_qkv[-1])
            grad_mixed = after(grad_mixed, grad_qkv[-1], *[line.payload for line in lines])
        part = attend_back(shift, ends, part, grad_mixed, log, first, count)
        grad_qkv.append(part)
    partials_one = heads_partials(jnp.concatenate(grad_qkv, 1), jnp.concatenate(qkv_w, 1), NT)
    got_one = heads_send(partials_one, got_forward)
    partials_one = lax.optimization_barrier(partials_one)
    sums.append(Weigh(normed_one, after(grad_qkv[-1], partials_one[-1]), (1, 0, 2)))
    hat_one, scale_one = norm_parts(rows_full)
    hats = jnp.split(hat_one, len(partials_one))
    grad_gain_one = sum(jnp.sum(p * h, 0) for p, h in zip(partials_one, hats))
    grad_shift_one = sum(jnp.sum(p, 0) for p in partials_one)
    grad_qkv_b = jnp.concatenate([jnp.sum(part, axis=0, dtype=F32) for part in grad_qkv]).reshape(pairs, 3, PAIR)

    wide = [
        v.reshape(blocks, depth)
        for v in (
            grad_gain_one,
            grad_shift_one,
            jnp.sum(grad_branch, axis=0, dtype=F32),
            grad_gain_two,
            grad_shift_two,
            jnp.sum(grad_out, axis=0, dtype=F32),
        )
    ]
    narrow = [
        jnp.swapaxes(v.reshape(heads, blocks, -1), 0, 1).reshape(blocks, -1)
        for v in (grad_up_b, grad_qkv_b[:, 0], grad_qkv_b[:, 2])
    ]
    packed = jnp.concatenate(wide + narrow, 1)
    used = packed.shape[1]
    padded = -(-used // 1024) * 1024
    packed = jnp.pad(packed, ((0, 0), (0, padded - used))).reshape(blocks * (padded // 128), 128)
    packed = Exchange(packed)
    lines = sums[::-1] + [up_sum, down_sum, out_sum]
    ended, count = [sums[-1].own], 0
    while lines:
        begun = []
        for line in lines:
            if line.order:
                begun.append(line.step(*ended))
            else:
                line.result = line.end(*ended)
        if count > 0 and packed.order:
            begun.append(packed.step(*ended))
        lines = [line for line in lines if line.result is None]
        ended, count = begun, count + 1
        if count == 2:
            got_one = after(got_one, *ended)
            ended = [got_one]
    while packed.order:
        packed.step()
    if lined() and width == 2 * PAIR * len(groups):
        *grad_qkv_w, grad_up_w = unpack(bit_of(3), [line.result for line in sums], up_sum.result)
    else:
        grad_up_w = joined(up_sum.result)
        grad_qkv_w = jnp.concatenate([joined(line.result) for line in sums], 1).reshape(depth, pairs, 3, PAIR)
        grad_qkv_w = [grad_qkv_w[:, :, k].reshape(depth, width) for k in range(3)]
    grad_out_w = joined(out_sum.result)
    grad_down_w = joined(down_sum.result)
    if paired():
        width_out = grad_out_w.shape[1] // 2
        grad_out_w = grad_out_w[:, :width_out] + swap(grad_out_w[:, width_out:])
    else:
        grad_out_w = lax.psum_scatter(grad_out_w, "heads", scatter_dimension=1, tiled=True)
    output = (own_rows(mid) + heads_sum(partials, got_forward) + down_b).astype(BF)
    grad_normed_one = heads_sum(partials_one, got_one)
    grad_input = grad_mid + norm_back(grad_normed_one, own_rows(hat_one), own_rows(scale_one), gain_one)
    packed = packed.take(()).reshape(-1)
    over_heads = packed[: 6 * depth].reshape(6, -1, depth // lax.axis_size("heads"))
    if paired():
        theirs = lax.dynamic_index_in_dim(over_heads, 1 - here, 1, keepdims=False)
        vector = lax.dynamic_index_in_dim(over_heads, here, 1, keepdims=False) + swap(theirs)
    else:
        vector = lax.psum(over_heads, "heads")
        vector = lax.dynamic_index_in_dim(vector, here, 1, keepdims=False)
    at = 6 * depth
    flat_grads = []
    for shard in (bias_up, bias_query, bias_value):
        flat_grads.append(packed[at : at + shard.size].reshape(shard.shape))
        at += shard.size
    return (
        output,
        grad_input,
        vector[0],
        vector[1],
        *grad_qkv_w,
        flat_grads[1],
        flat_grads[2],
        grad_out_w.T,
        vector[2],
        vector[3],
        vector[4],
        grad_up_w,
        flat_grads[0],
        grad_down_w.T,
        vector[5],
    )


def solution(mesh):
    in_specs = (
        P(("fsdp", "heads"), None),
        P("fsdp"),
        P("fsdp"),
        P("fsdp", "heads"),
        P("fsdp", "heads"),
        P("fsdp", "heads"),
        P("heads", "fsdp"),
        P("heads", "fsdp"),
        P("heads", "fsdp"),
        P("fsdp"),
        P("fsdp"),
        P("fsdp"),
        P("fsdp", "heads"),
        P("heads", "fsdp"),
        P("heads", "fsdp"),
        P("fsdp"),
        P(("fsdp", "heads"), None),
        P("fsdp", None),
    )
    out_specs = (
        P(("fsdp", "heads"), None),
        P(("fsdp", "heads"), None),
        P(("fsdp", "heads")),
        P(("fsdp", "heads")),
        P("fsdp", "heads"),
        P("fsdp", "heads"),
        P("fsdp", "heads"),
        P("heads", "fsdp"),
        P("heads", "fsdp"),
        P("heads", "fsdp"),
        P(("fsdp", "heads")),
        P(("fsdp", "heads")),
        P(("fsdp", "heads")),
        P("fsdp", "heads"),
        P("heads", "fsdp"),
        P("heads", "fsdp"),
        P(("fsdp", "heads")),
    )
    return jax.shard_map(local, mesh=mesh, in_specs=in_specs, out_specs=out_specs, check_vma=False)
```

```python
import functools

import jax
import jax.numpy as jnp
from jax import lax
from jax.experimental import pallas as pl
from jax.experimental.pallas import tpu as pltpu
from jax.sharding import PartitionSpec as P

HD = 64
PAIR = 2 * HD
EPSILON = 1e-05
GELU_SCALE = 0.7978845608028654
MASKED = -1e30
F32 = jnp.float32
BF = jnp.bfloat16
NN = (((1,), (0,)), ((), ()))
NT = (((1,), (1,)), ((), ()))
TN = (((0,), (0,)), ((), ()))


def dot(left, right, dims=NN):
    return lax.dot_general(left, right, dims, preferred_element_type=F32)


def starts_of(ends_ref, position):
    start = jnp.zeros_like(position)
    for slot in range(ends_ref.shape[0]):
        start = jnp.where(position >= ends_ref[slot], ends_ref[slot], start)
    return start


def place(block, step, shift, rows):
    return pl.ds(pl.multiple_of(lax.rem(block * step + shift, rows), step), step)


def attend_kernel(rows, step, shift_ref, ends_ref, qkv_ref, mixed_ref, turned_ref, log_ref, keys, values, bias):
    shift = shift_ref[0]

    @pl.when(pl.program_id(0) == 0)
    def _():
        for i in range(rows // step):
            wide = (i + 1) * step
            row = lax.broadcasted_iota(jnp.int32, (step, 1), 0) + i * step
            column = lax.broadcasted_iota(jnp.int32, (step, wide), 1)
            seen = (column >= starts_of(ends_ref, row)) & (column <= row)
            bias[i * step : wide, :wide] = jnp.where(seen, 0.0, MASKED)

    for b in range(rows // step):
        keys[b * step : (b + 1) * step, :] = qkv_ref[place(b, step, shift, rows), PAIR : 2 * PAIR]
        values[b * step : (b + 1) * step, :] = qkv_ref[place(b, step, shift, rows), 2 * PAIR :]
    lane = lax.broadcasted_iota(jnp.int32, (step, PAIR), 1)
    second = lane >= HD
    for i in range(rows // step):
        wide = (i + 1) * step
        query = qkv_ref[place(i, step, shift, rows), :PAIR] * jnp.asarray(HD**-0.5, BF)
        mixed, logs = [], []
        for h in range(2):
            own = jnp.where(second == (h == 1), query, jnp.zeros_like(query))
            scores = dot(own, keys[:wide, :], NT) + bias[i * step : wide, :wide]
            top = jnp.max(scores, axis=1, keepdims=True)
            weights = jnp.exp(scores - top)
            total = jnp.sum(weights, axis=1, keepdims=True)
            mixed.append(dot(weights.astype(BF), values[:wide, :]) * (1.0 / total))
            logs.append(top + jnp.log(total))
        mixed = jnp.where(second, mixed[1], mixed[0]).astype(BF)
        mixed_ref[place(i, step, shift, rows), :] = mixed
        turned_ref[place(i, step, shift + rows // 2, rows), :] = mixed
        log_ref[0, :, i * step : wide] = jnp.transpose(jnp.where(lane >= 4, logs[1], logs[0]))[:8]


def attend_back_kernel(
    rows, step, shift_ref, ends_ref, qkv_ref, grad_ref, log_ref, out_ref, keys, values, bias, key_sum, value_sum
):
    shift = shift_ref[0]

    @pl.when(pl.program_id(0) == 0)
    def _():
        for i in range(rows // step):
            wide = (i + 1) * step
            row = lax.broadcasted_iota(jnp.int32, (1, step), 1) + i * step
            column = lax.broadcasted_iota(jnp.int32, (wide, step), 0)
            seen = (column >= starts_of(ends_ref, row)) & (column <= row)
            bias[:wide, i * step : wide] = jnp.where(seen, 0.0, MASKED)

    for b in range(rows // step):
        keys[b * step : (b + 1) * step, :] = qkv_ref[place(b, step, shift, rows), PAIR : 2 * PAIR]
        values[b * step : (b + 1) * step, :] = qkv_ref[place(b, step, shift, rows), 2 * PAIR :]
    second = lax.broadcasted_iota(jnp.int32, (step, PAIR), 1) >= HD
    for i in reversed(range(rows // step)):
        low, wide = i * step, (i + 1) * step
        query = qkv_ref[place(i, step, shift, rows), :PAIR] * jnp.asarray(HD**-0.5, BF)
        grad = grad_ref[place(i, step, shift, rows), :]
        to_query, to_key, to_value = [], [], []
        for h in range(2):
            own_query = jnp.where(second == (h == 1), query, jnp.zeros_like(query))
            own_grad = jnp.where(second == (h == 1), grad, jnp.zeros_like(grad))
            scores = dot(keys[:wide, :], own_query, NT) + bias[:wide, low:wide]
            probs = jnp.exp(scores - log_ref[0, 4 * h : 4 * h + 1, low:wide])
            grad_probs = dot(values[:wide, :], own_grad, NT)
            spread = jnp.sum(probs * grad_probs, axis=0, keepdims=True)
            grad_scores = (probs * (grad_probs - spread)).astype(BF)
            to_value.append(dot(probs.astype(BF), own_grad))
            to_key.append(dot(grad_scores, own_query))
            to_query.append(dot(grad_scores, keys[:wide, :], TN))
        grad_query = jnp.where(second, to_query[1], to_query[0]) * (HD**-0.5)
        grad_key = to_key[0] + to_key[1]
        grad_value = to_value[0] + to_value[1]
        if wide < rows:
            grad_key = grad_key + key_sum[:wide, :]
            grad_value = grad_value + value_sum[:wide, :]
        out_ref[place(i, step, shift, rows), :PAIR] = grad_query.astype(BF)
        out_ref[place(i, step, shift, rows), PAIR : 2 * PAIR] = grad_key[low:, :].astype(BF)
        out_ref[place(i, step, shift, rows), 2 * PAIR :] = grad_value[low:, :].astype(BF)
        if low > 0:
            key_sum[:low, :] = grad_key[:low, :]
            value_sum[:low, :] = grad_value[:low, :]


def attend(shift, ends, qkv, pairs):
    rows = qkv.shape[0]
    step = min(256, rows)
    work = 2 * pairs * rows * rows
    return pl.pallas_call(
        functools.partial(attend_kernel, rows, step),
        grid_spec=pltpu.PrefetchScalarGridSpec(
            num_scalar_prefetch=2,
            grid=(pairs,),
            in_specs=[pl.BlockSpec((rows, 3 * PAIR), lambda p, *_: (0, p))],
            out_specs=[
                pl.BlockSpec((rows, PAIR), lambda p, *_: (0, p)),
                pl.BlockSpec((rows, PAIR), lambda p, *_: (0, p)),
                pl.BlockSpec((1, 8, rows), lambda p, *_: (p, 0, 0)),
            ],
            scratch_shapes=[
                pltpu.VMEM((rows, PAIR), BF),
                pltpu.VMEM((rows, PAIR), BF),
                pltpu.VMEM((rows, rows), F32),
            ],
        ),
        out_shape=[
            jax.ShapeDtypeStruct((rows, PAIR * pairs), BF),
            jax.ShapeDtypeStruct((rows, PAIR * pairs), BF),
            jax.ShapeDtypeStruct((pairs, 8, rows), F32),
        ],
        compiler_params=pltpu.CompilerParams(vmem_limit_bytes=40 << 20),
        cost_estimate=pl.CostEstimate(
            flops=work * 128, bytes_accessed=rows * PAIR * pairs * 8, transcendentals=0
        ),
        name="attend",
    )(shift, ends, qkv)


def attend_back(shift, ends, qkv, grad_mixed, logs, first, pairs):
    rows = qkv.shape[0]
    step = min(256, rows)
    work = 2 * pairs * rows * rows
    return pl.pallas_call(
        functools.partial(attend_back_kernel, rows, step),
        grid_spec=pltpu.PrefetchScalarGridSpec(
            num_scalar_prefetch=2,
            grid=(pairs,),
            in_specs=[
                pl.BlockSpec((rows, 3 * PAIR), lambda p, *_: (0, p)),
                pl.BlockSpec((rows, PAIR), lambda p, *_: (0, p + first)),
                pl.BlockSpec((1, 8, rows), lambda p, *_: (p, 0, 0)),
            ],
            out_specs=pl.BlockSpec((rows, 3 * PAIR), lambda p, *_: (0, p)),
            scratch_shapes=[
                pltpu.VMEM((rows, PAIR), BF),
                pltpu.VMEM((rows, PAIR), BF),
                pltpu.VMEM((rows, rows), F32),
                pltpu.VMEM((rows, PAIR), F32),
                pltpu.VMEM((rows, PAIR), F32),
            ],
        ),
        out_shape=jax.ShapeDtypeStruct((rows, 3 * PAIR * pairs), BF),
        compiler_params=pltpu.CompilerParams(vmem_limit_bytes=40 << 20),
        cost_estimate=pl.CostEstimate(
            flops=work * 256, bytes_accessed=rows * PAIR * pairs * 14, transcendentals=0
        ),
        name="attend_back",
    )(shift, ends, qkv, grad_mixed, logs)


def norm_kernel(parts, gain_ref, shift_ref, *refs):
    part = pl.program_id(0) // (pl.num_programs(0) // parts)
    for i in range(parts):

        @pl.when(part == i)
        def _(i=i):
            rows = refs[i][...].astype(F32)
            centered = rows - jnp.mean(rows, axis=-1, keepdims=True)
            scale = lax.rsqrt(jnp.mean(centered * centered, axis=-1, keepdims=True) + EPSILON)
            refs[parts][...] = (centered * scale * gain_ref[...] + shift_ref[...]).astype(BF)


def norm_all(arrays, gain, shift):
    share, width = arrays[0].shape
    step = min(256, share)
    per, parts = share // step, len(arrays)
    line = pl.BlockSpec((1, width), lambda i: (0, 0))
    return pl.pallas_call(
        functools.partial(norm_kernel, parts),
        grid=(per * parts,),
        in_specs=[line, line]
        + [
            pl.BlockSpec((step, width), lambda i, k=k: (jnp.clip(i - k * per, 0, per - 1), 0))
            for k in range(parts)
        ],
        out_specs=pl.BlockSpec((step, width), lambda i: (i, 0)),
        out_shape=jax.ShapeDtypeStruct((share * parts, width), BF),
        compiler_params=pltpu.CompilerParams(vmem_limit_bytes=32 << 20),
        cost_estimate=pl.CostEstimate(flops=0, bytes_accessed=share * parts * width * 4, transcendentals=0),
        name="norm_all",
    )(gain, shift, *arrays)


def spread_kernel(depth, units, each, pairs, flat_ref, wide_ref, up_ref, qkv_ref):
    devices = flat_ref.shape[0]

    def laid(row, lane, size):
        total = devices * size
        source = flat_ref[:, row, :]
        at = lax.broadcasted_iota(jnp.int32, (128, total), 1) & (size - 1)
        pick = (lax.broadcasted_iota(jnp.int32, (128, total), 0) == at + lane).astype(BF)
        owner = lax.broadcasted_iota(jnp.int32, (devices, total), 1) // size
        mine = owner == lax.broadcasted_iota(jnp.int32, (devices, total), 0)
        return jnp.sum(jnp.where(mine, dot(source, pick), 0.0), axis=0, keepdims=True)

    for i in range(6):
        wide_ref[i : i + 1, :] = laid(i, 0, depth)
    for h in range(2 * pairs):
        up_ref[:, h * devices * units : (h + 1) * devices * units] = laid(8 + h, 0, units)
    for p in range(pairs):
        for k in range(3):
            column = (3 * p + k) * PAIR
            if k == 1:
                qkv_ref[:, column : column + PAIR] = jnp.zeros((1, PAIR), F32)
                continue
            lane = units + (each if k == 2 else 0)
            halves = [laid(8 + 2 * p + h, lane, each) for h in range(2)]
            qkv_ref[:, column : column + PAIR] = jnp.concatenate(halves, 1)


def spread(flat, depth, units, each, pairs):
    devices = flat.shape[0]
    shapes = [(6, devices * depth), (1, 2 * pairs * devices * units), (1, 3 * PAIR * pairs)]
    return pl.pallas_call(
        functools.partial(spread_kernel, depth, units, each, pairs),
        out_shape=[jax.ShapeDtypeStruct(shape, F32) for shape in shapes],
        compiler_params=pltpu.CompilerParams(vmem_limit_bytes=32 << 20),
        name="spread",
    )(flat)


def feed_kernel(normed_ref, grad_ref, up_ref, down_ref, bias_ref, hidden_ref, out_ref, sum_ref):
    step = min(256, normed_ref.shape[0])
    total = None
    for i in range(normed_ref.shape[0] // step):
        rows = slice(i * step, (i + 1) * step)
        pre = dot(normed_ref[rows, :], up_ref[...]) + bias_ref[...]
        squared = pre * pre
        bend = 0.5 + 0.5 * jnp.tanh(pre * (GELU_SCALE + (GELU_SCALE * 0.044715) * squared))
        hidden = pre * bend
        hidden_ref[rows, :] = hidden.astype(BF)
        slope = bend + hidden * (1.0 - bend) * (2 * GELU_SCALE + (6 * GELU_SCALE * 0.044715) * squared)
        grad = (slope * dot(grad_ref[rows, :], down_ref[...])).astype(BF)
        out_ref[rows, :] = grad
        part = jnp.sum(grad.astype(F32), axis=0, keepdims=True)
        total = part if total is None else total + part
    sum_ref[...] = total


def feed(normed, grad_out, up_w, down_w, up_b):
    rows, width = normed.shape
    units = up_w.shape[1]
    step = min(512, units)
    whole = pl.BlockSpec((rows, width), lambda i: (0, 0))
    columns = pl.BlockSpec((width, step), lambda i: (0, i))
    line = pl.BlockSpec((1, step), lambda i: (0, i))
    out = pl.BlockSpec((rows, step), lambda i: (0, i))
    return pl.pallas_call(
        feed_kernel,
        grid=(units // step,),
        in_specs=[whole, whole, columns, columns, line],
        out_specs=[out, out, line],
        out_shape=[
            jax.ShapeDtypeStruct((rows, units), BF),
            jax.ShapeDtypeStruct((rows, units), BF),
            jax.ShapeDtypeStruct((1, units), F32),
        ],
        compiler_params=pltpu.CompilerParams(vmem_limit_bytes=44 << 20),
        cost_estimate=pl.CostEstimate(flops=rows * units * width, bytes_accessed=1 << 20, transcendentals=0),
        name="feed",
    )(normed, grad_out, up_w, down_w, up_b)


BITS = 4


def lined():
    return lax.axis_size("fsdp") == 1 << BITS


def bit_of(axis):
    return (lax.axis_index("fsdp") >> (BITS - 1 - axis)) & 1


def trade(array, axis):
    flip = 1 << (BITS - 1 - axis)
    return lax.ppermute(array, "fsdp", [(i, i ^ flip) for i in range(1 << BITS)])


def after(array, *earlier):
    earlier = tuple(e for e in earlier if e is not None)
    return lax.optimization_barrier((array,) + earlier)[0] if earlier else array


def interleave_kernel(core_ref, own_ref, other_ref, out_ref):
    core = core_ref[0]
    for i in range(own_ref.shape[0]):
        out_ref[i, core] = own_ref[i]
        out_ref[i, 1 - core] = other_ref[i]


def interleave(core, own, other):
    n, r, c = own.shape
    per = 2
    spec = pl.BlockSpec((per, r, c), lambda i, *_: (i, 0, 0))
    return pl.pallas_call(
        interleave_kernel,
        grid_spec=pltpu.PrefetchScalarGridSpec(
            num_scalar_prefetch=1,
            grid=(n // per,),
            in_specs=[spec, spec],
            out_specs=pl.BlockSpec((per, 2, r, c), lambda i, *_: (i, 0, 0, 0)),
        ),
        out_shape=jax.ShapeDtypeStruct((n, 2, r, c), own.dtype),
        compiler_params=pltpu.CompilerParams(vmem_limit_bytes=32 << 20),
        cost_estimate=pl.CostEstimate(flops=0, bytes_accessed=own.size * 8, transcendentals=0),
        name="interleave",
    )(core.reshape(1).astype(jnp.int32), own, other)


def placed(parts):
    array, other, axis, at = parts
    if other is None:
        return array
    return jnp.where(bit_of(axis) == 1, jnp.stack([other, array], at), jnp.stack([array, other], at))


class Gather:
    def __init__(self, shard, order=(0, 1, 2)):
        self.parts, self.order, self.passed, self.width = (shard, None, 0, 0), list(order), [], shard.shape[1]
        self.payload = None

    def take(self, earlier):
        array, other, axis, at = self.parts
        if other is None:
            return after(array, *earlier)
        array, other = after((array, other), *earlier)
        return placed((array, other, axis, at))

    def step(self, *earlier):
        block = self.take(earlier)
        if not lined():
            if not self.passed:
                block = lax.all_gather(block, "fsdp", axis=0, tiled=True)
                self.parts, self.passed = (block, None, 0, 0), [0]
            return block
        axis = self.order.pop(0)
        at = sum(p < axis for p in self.passed)
        self.passed.append(axis)
        self.payload = block
        other = trade(block, axis)
        self.parts = (block, other, axis, at)
        return other

    def end(self, *earlier):
        if not lined():
            return self.step(*earlier)
        while self.order:
            self.step(*earlier)
        block = self.take(earlier).reshape(8, -1, self.width)
        other = trade(block, 3)
        if block.shape[1] * self.width < 1 << 15:
            whole = placed((block, other, 3, 1))
        else:
            whole = interleave(bit_of(3), block, other)
        return whole.reshape(-1, self.width)


def at_index(array, index, axis):
    return lax.dynamic_index_in_dim(array, index, axis, keepdims=False)


class Halver:
    def __init__(self, parts, axes, order, last):
        self.own, self.got, self.left, self.order, self.last = parts, None, list(axes), list(order), last
        self.payload, self.result = None, None

    def take(self, earlier):
        if self.got is None:
            return after(self.own, *earlier)
        own, got = after((self.own, self.got), *earlier)
        total = own.astype(F32) + got.astype(F32)
        return total if not self.order and self.last else total.astype(own.dtype)

    def step(self, *earlier):
        if not self.order:
            return None
        axis = self.order[0]
        at = self.left.index(axis)
        parts = self.take(earlier)
        self.order.pop(0)
        self.left.remove(axis)
        mine = bit_of(axis)
        self.payload = at_index(parts, 1 - mine, at)
        self.got = trade(self.payload, axis)
        self.own = at_index(parts, mine, at)
        return self.got


class Exchange:
    def __init__(self, whole):
        self.rows, self.got, self.payload, self.result = whole.shape[0], None, None, None
        if lined():
            self.own, self.order = whole.reshape((4, 4, -1) + whole.shape[1:]), [1, 0]
        else:
            self.own, self.order = lax.psum_scatter(whole, "fsdp", scatter_dimension=0, tiled=True), []

    def take(self, earlier):
        own, got = after((self.own, tuple(self.got or ())), *earlier)
        return own + sum(got) if got else own

    def step(self, *earlier):
        parts = self.take(earlier)
        at = self.order.pop(0)
        mine = (lax.axis_index("fsdp") >> (0 if at else 2)) & 3
        self.own = at_index(parts, mine, at)
        self.got = []
        for flip in range(1, 4):
            pairs = [(i, i ^ (flip << (0 if at else 2))) for i in range(16)]
            self.got.append(lax.ppermute(at_index(parts, mine ^ flip, at), "fsdp", pairs))
        return self.got[-1]


def columns_of(array, index):
    width = array.shape[1] // 2
    return lax.dynamic_slice_in_dim(array, index * width, width, 1)


class Weigh(Halver):
    def __init__(self, left, right, order=(2, 1, 0)):
        if not lined():
            total = lax.psum_scatter(dot(left, right, TN).astype(BF), "fsdp", scatter_dimension=0, tiled=True)
            super().__init__(total.astype(F32), (), (), True)
            return
        core = bit_of(3)
        got = trade(dot(left, columns_of(right, 1 - core), TN).astype(BF), 3)
        total = (dot(left, columns_of(right, core), TN) + got.astype(F32)).astype(BF)
        super().__init__(total.reshape(2, 2, 2, -1, total.shape[1]), (0, 1, 2), order, True)

    def end(self, *earlier):
        total = self.take(earlier)
        if not lined():
            return total
        core = bit_of(3)
        total = total.reshape(2, -1, total.shape[1])
        got = trade(at_index(total, 1 - core, 0).astype(BF), 3)
        return at_index(total, core, 0), got


def joined(result):
    if not lined():
        return result
    own, got = result[0], result[1].astype(F32)
    return jnp.where(bit_of(3) == 1, jnp.concatenate([got, own], 1), jnp.concatenate([own, got], 1))


def unpack_kernel(count, core_ref, *refs):
    core = core_ref[0]
    for g in range(count):
        for half, part in enumerate(refs[2 * g : 2 * g + 2]):
            pair = 2 * g + (core if half == 0 else 1 - core)
            columns = pl.ds(pl.multiple_of(pair * PAIR, PAIR), PAIR)
            for k in range(3):
                refs[2 * count + 2 + k][:, columns] = part[:, k * PAIR : (k + 1) * PAIR].astype(F32)
    width = refs[2 * count].shape[1]
    for half in range(2):
        place_at = core if half == 0 else 1 - core
        columns = pl.ds(pl.multiple_of(place_at * width, 128), width)
        refs[2 * count + 5][:, columns] = refs[2 * count + half][...].astype(F32)


def unpack(core, groups, up):
    rows, width = groups[0][0].shape[0], len(groups) * 2 * PAIR
    shapes = [(rows, width)] * 3 + [(rows, 2 * up[0].shape[1])]
    return pl.pallas_call(
        functools.partial(unpack_kernel, len(groups)),
        in_specs=[pl.BlockSpec(memory_space=pltpu.SMEM)]
        + [pl.BlockSpec(memory_space=pltpu.VMEM)] * (2 * len(groups) + 2),
        out_specs=[pl.BlockSpec(memory_space=pltpu.VMEM)] * 4,
        out_shape=[jax.ShapeDtypeStruct(shape, F32) for shape in shapes],
        compiler_params=pltpu.CompilerParams(vmem_limit_bytes=32 << 20),
        name="unpack",
    )(core.reshape(1).astype(jnp.int32), *[half for group in groups for half in group], *up)


def pack_kernel(counts, *refs):
    weights, outs, pair = refs[:3], refs[3:], 0
    for out, count in zip(outs, counts):
        for p in range(count):
            for k in range(3):
                column = (3 * p + k) * PAIR
                out[:, column : column + PAIR] = weights[k][:, pair * PAIR : (pair + 1) * PAIR]
            pair += 1


def pack(weights, counts):
    rows = weights[0].shape[0]
    return pl.pallas_call(
        functools.partial(pack_kernel, counts),
        out_shape=[jax.ShapeDtypeStruct((rows, 3 * PAIR * count), BF) for count in counts],
        compiler_params=pltpu.CompilerParams(vmem_limit_bytes=32 << 20),
        name="pack",
    )(*weights)


def lines_kernel(*refs):
    lines, out, rows = refs[:-2], refs[-2], refs[-1]
    rows[...] = jnp.zeros_like(rows)
    for i, line in enumerate(lines[:6]):
        rows[i : i + 1, : line.shape[1]] = line[...].astype(F32)
    lane = 0
    for line in lines[6:]:
        rows[8 : 8 + line.shape[0], lane : lane + line.shape[1]] = line[...].astype(F32)
        lane += line.shape[1]
    out[...] = rows[...].astype(BF)


def pack_lines(lines):
    return pl.pallas_call(
        lines_kernel,
        out_shape=jax.ShapeDtypeStruct((16, 128), BF),
        scratch_shapes=[pltpu.VMEM((16, 128), F32)],
        compiler_params=pltpu.CompilerParams(vmem_limit_bytes=32 << 20),
        name="pack_lines",
    )(*lines)


def paired():
    return lax.axis_size("heads") == 2


def swap(array):
    return lax.ppermute(array, "heads", [(0, 1), (1, 0)])


def heads_rows(share):
    if not paired():
        return lax.all_gather(share, "heads", axis=0, tiled=True)
    return jnp.concatenate([share, swap(share)], 0)


def heads_columns(share):
    if not paired():
        return lax.all_gather(share, "heads", axis=1, tiled=True)
    return jnp.concatenate([share, swap(share)], 1)


def heads_partials(left, right, dims):
    if not paired():
        return [dot(left, right, dims)]
    share = left.shape[0] // 2
    theirs = dot(left[share:], right, dims)
    return [dot(left[:share], right, dims), theirs]


def heads_send(partials, *earlier):
    if not paired():
        partial = after(partials[0].astype(BF), *earlier)
        return lax.psum_scatter(partial, "heads", scatter_dimension=0, tiled=True)
    return swap(after(partials[1].astype(BF), *earlier))


def heads_sum(partials, got):
    return partials[0].astype(F32) + got.astype(F32) if paired() else got.astype(F32)


def heads_exchange(columns):
    if not paired():
        return lax.all_to_all(columns, "heads", 1, 0, tiled=True)
    width = columns.shape[1] // 2
    return jnp.concatenate([columns[:, :width], swap(columns[:, width:])], 0)


def norm_parts(rows):
    mean = jnp.mean(rows, axis=-1, keepdims=True)
    centered = rows - mean
    scale = lax.rsqrt(jnp.mean(centered * centered, axis=-1, keepdims=True) + EPSILON)
    return centered * scale, scale


def norm_back(grad, hat, scale, gain):
    e = grad * gain
    return scale * (e - jnp.mean(e, -1, keepdims=True) - hat * jnp.mean(e * hat, -1, keepdims=True))


def local(
    tokens,
    ln1_gain,
    ln1_bias,
    w_query,
    w_key,
    w_value,
    bias_query,
    bias_value,
    w_out,
    bias_out,
    ln2_gain,
    ln2_bias,
    w_up,
    bias_up,
    w_down,
    bias_down,
    cotangent,
    seq_lengths,
):
    share = tokens.shape[0]
    rows = share * lax.axis_size("heads")
    depth = ln1_gain.shape[0]
    width = w_query.shape[1]
    pairs = width // PAIR
    groups = [(0, pairs)] if pairs < 2 else [(0, pairs // 2), (pairs // 2, pairs - pairs // 2)]
    here = lax.axis_index("heads")
    shift = (here * share if paired() else jnp.zeros((), jnp.int32)).astype(jnp.int32).reshape(1)
    ends = jnp.cumsum(seq_lengths[0]).astype(jnp.int32)
    live = (here * share + jnp.arange(share, dtype=jnp.int32) < ends[-1]).astype(F32)

    blocks, heads, units, each = lax.axis_size("fsdp"), bias_query.shape[0], bias_up.shape[1], bias_query.shape[1]
    shards = [Gather(a) for a in pack((w_query, w_key, w_value), [count for _, count in groups])]
    vectors = (ln1_gain, ln1_bias, bias_out, ln2_gain, ln2_bias, bias_down)
    lines = [v.reshape(1, depth) for v in after(vectors, shards[0].parts[0])] + [bias_up, bias_query, bias_value]
    small = Gather(pack_lines(lines))
    tokens_other = swap(tokens) if paired() else None
    out_shard = Gather(heads_columns(w_out.T))
    up_shard = Gather(w_up)
    down_shard = Gather(w_down.T)
    full_width = out_shard.width
    rounds = lined() and len(shards) == 2
    if rounds:
        ended = [shards[0].step(), small.step()]
        ended = [shards[0].step(*ended), small.step(*ended), shards[1].step(*ended)]
        ended += [tokens_other]
        ended = [shards[0].step(*ended), small.step(*ended), shards[1].step(*ended), out_shard.step(*ended)]
        qkv_w = [shards[0].end(*ended)]
        flat = small.end(*ended)
        ended = [shards[1].step(*ended), out_shard.step(*ended), up_shard.step(*ended)]
    else:
        qkv_w = [shard.end() for shard in shards]
        flat = small.end()
    vectors, up_b, qkv_b = spread(flat.reshape(blocks, -1, 128), depth, units, each, pairs)
    gain_one, shift_one, out_b, gain_two, shift_two, down_b = [vectors[i : i + 1] for i in range(6)]

    grad_out = (cotangent.astype(F32) * live[:, None]).astype(BF)
    grad_out_full = heads_rows(after(grad_out, tokens_other))
    if paired():
        rows_full = jnp.concatenate([tokens, tokens_other], 0).astype(F32)
    else:
        rows_full = lax.all_gather(tokens, "heads", axis=0, tiled=True).astype(F32)
    own_rows = lambda array: lax.dynamic_slice_in_dim(array, 0 if paired() else here * share, share, 0)
    normed_one = norm_all([tokens, tokens_other] if paired() else [rows_full], gain_one, shift_one)
    mixed, others, logs, qkv = [], [], [], []
    for g, (first, count) in enumerate(groups):
        bias = qkv_b[:, first * 3 * PAIR : (first + count) * 3 * PAIR]
        projected = (dot(normed_one, qkv_w[g]) + bias).astype(BF)
        if rounds and g == 0:
            projected = after(projected, *ended)
            qkv_w.append(shards[1].end(projected))
            out_shard.step(projected)
            up_shard.step(projected)
            down_shard.step(projected)
            projected = after(projected, out_shard.payload, up_shard.payload)
        elif rounds:
            up_shard.step(mixed[0])
            down_shard.step(mixed[0])
            projected = after(projected, up_shard.payload, down_shard.payload)
        qkv.append(projected)
        part, turned, log = attend(shift, ends, projected, count)
        mixed.append(part)
        logs.append(log)
        if paired():
            others.append(swap(after(turned, others[-1] if others else grad_out_full)))
    down_shard.step(mixed[-1])
    out_w = out_shard.end(mixed[-1])
    up_w = up_shard.end(out_w)
    down_w = down_shard.end(out_w)
    mixed = jnp.concatenate(mixed, 1)
    if paired():
        mixed_full = jnp.concatenate([mixed] + others, 1)
    else:
        mixed_full = lax.all_gather(mixed, "heads", axis=1, tiled=True)
    mid = rows_full + dot(mixed_full, out_w, NT) + out_b
    hat_two, scale_two = norm_parts(mid)
    normed_two = (hat_two * gain_two + shift_two).astype(BF)

    hidden, grad_pre, grad_up_b = feed(normed_two, grad_out_full, up_w, down_w, up_b)
    partials_two = heads_partials(grad_pre, up_w, NT)
    got_two = heads_send(partials_two)
    down_sum = Weigh(grad_out_full, hidden)
    up_sum = Weigh(normed_two, grad_pre, (1, 0, 2))
    down_sum.step()
    grad_mid = grad_out.astype(F32) + norm_back(
        heads_sum(partials_two, after(got_two, up_sum.own, down_sum.payload)), own_rows(hat_two), own_rows(scale_two), gain_two
    )
    grad_branch = grad_mid.astype(BF)
    up_sum.step()
    mixing = heads_exchange(dot(after(grad_branch, up_sum.payload), out_w).astype(BF))
    out_sum = Weigh(grad_branch, own_rows(mixed_full))
    partials = lax.optimization_barrier(heads_partials(hidden, down_w, NT))
    hats = jnp.split(hat_two, len(partials_two))
    grad_gain_two = sum(jnp.sum(p * h, 0) for p, h in zip(partials_two, hats))
    grad_shift_two = sum(jnp.sum(p, 0) for p in partials_two)

    out_sum.step()
    grad_mixed = after(mixing, out_sum.own, out_sum.payload, grad_gain_two, grad_shift_two)
    got_forward = heads_send(partials, mixing)
    grad_qkv, sums = [], []
    for g, ((first, count), log, part) in enumerate(zip(groups, logs, qkv)):
        if g > 0:
            sums.append(Weigh(normed_one, grad_qkv[-1]))
            lines = [sums[-1], up_sum, down_sum, out_sum]
            for line in lines:
                line.step(grad_qkv[-1])
            grad_mixed = after(grad_mixed, grad_qkv[-1], *[line.payload for line in lines])
        part = attend_back(shift, ends, part, grad_mixed, log, first, count)
        grad_qkv.append(part)
    partials_one = heads_partials(jnp.concatenate(grad_qkv, 1), jnp.concatenate(qkv_w, 1), NT)
    got_one = heads_send(partials_one, got_forward)
    partials_one = lax.optimization_barrier(partials_one)
    sums.append(Weigh(normed_one, after(grad_qkv[-1], partials_one[-1])))
    hat_one, scale_one = norm_parts(rows_full)
    hats = jnp.split(hat_one, len(partials_one))
    grad_gain_one = sum(jnp.sum(p * h, 0) for p, h in zip(partials_one, hats))
    grad_shift_one = sum(jnp.sum(p, 0) for p in partials_one)
    grad_qkv_b = jnp.concatenate([jnp.sum(part, axis=0, dtype=F32) for part in grad_qkv]).reshape(pairs, 3, PAIR)

    wide = [
        v.reshape(blocks, depth)
        for v in (
            grad_gain_one,
            grad_shift_one,
            jnp.sum(grad_branch, axis=0, dtype=F32),
            grad_gain_two,
            grad_shift_two,
            jnp.sum(grad_out, axis=0, dtype=F32),
        )
    ]
    narrow = [
        jnp.swapaxes(v.reshape(heads, blocks, -1), 0, 1).reshape(blocks, -1)
        for v in (grad_up_b, grad_qkv_b[:, 0], grad_qkv_b[:, 2])
    ]
    packed = jnp.concatenate(wide + narrow, 1)
    used = packed.shape[1]
    padded = -(-used // 1024) * 1024
    packed = jnp.pad(packed, ((0, 0), (0, padded - used))).reshape(blocks * (padded // 128), 128)
    packed = Exchange(packed)
    lines = sums[::-1] + [up_sum, down_sum, out_sum]
    ended, count = [sums[-1].own], 0
    while lines:
        begun = []
        for line in lines:
            if line.order:
                begun.append(line.step(*ended))
            else:
                line.result = line.end(*ended)
        if count > 0 and packed.order:
            begun.append(packed.step(*ended))
        lines = [line for line in lines if line.result is None]
        ended, count = begun, count + 1
        if count == 2:
            got_one = after(got_one, *ended)
            ended = [got_one]
    while packed.order:
        packed.step()
    if lined() and width == 2 * PAIR * len(groups):
        *grad_qkv_w, grad_up_w = unpack(bit_of(3), [line.result for line in sums], up_sum.result)
    else:
        grad_up_w = joined(up_sum.result)
        grad_qkv_w = jnp.concatenate([joined(line.result) for line in sums], 1).reshape(depth, pairs, 3, PAIR)
        grad_qkv_w = [grad_qkv_w[:, :, k].reshape(depth, width) for k in range(3)]
    grad_out_w = joined(out_sum.result)
    grad_down_w = joined(down_sum.result)
    if paired():
        width_out = grad_out_w.shape[1] // 2
        grad_out_w = grad_out_w[:, :width_out] + swap(grad_out_w[:, width_out:])
    else:
        grad_out_w = lax.psum_scatter(grad_out_w, "heads", scatter_dimension=1, tiled=True)
    output = (own_rows(mid) + heads_sum(partials, got_forward) + down_b).astype(BF)
    grad_normed_one = heads_sum(partials_one, got_one)
    grad_input = grad_mid + norm_back(grad_normed_one, own_rows(hat_one), own_rows(scale_one), gain_one)
    packed = packed.take(()).reshape(-1)
    over_heads = packed[: 6 * depth].reshape(6, -1, depth // lax.axis_size("heads"))
    if paired():
        theirs = lax.dynamic_index_in_dim(over_heads, 1 - here, 1, keepdims=False)
        vector = lax.dynamic_index_in_dim(over_heads, here, 1, keepdims=False) + swap(theirs)
    else:
        vector = lax.psum(over_heads, "heads")
        vector = lax.dynamic_index_in_dim(vector, here, 1, keepdims=False)
    at = 6 * depth
    flat_grads = []
    for shard in (bias_up, bias_query, bias_value):
        flat_grads.append(packed[at : at + shard.size].reshape(shard.shape))
        at += shard.size
    return (
        output,
        grad_input,
        vector[0],
        vector[1],
        *grad_qkv_w,
        flat_grads[1],
        flat_grads[2],
        grad_out_w.T,
        vector[2],
        vector[3],
        vector[4],
        grad_up_w,
        flat_grads[0],
        grad_down_w.T,
        vector[5],
    )


def solution(mesh):
    in_specs = (
        P(("fsdp", "heads"), None),
        P("fsdp"),
        P("fsdp"),
        P("fsdp", "heads"),
        P("fsdp", "heads"),
        P("fsdp", "heads"),
        P("heads", "fsdp"),
        P("heads", "fsdp"),
        P("heads", "fsdp"),
        P("fsdp"),
        P("fsdp"),
        P("fsdp"),
        P("fsdp", "heads"),
        P("heads", "fsdp"),
        P("heads", "fsdp"),
        P("fsdp"),
        P(("fsdp", "heads"), None),
        P("fsdp", None),
    )
    out_specs = (
        P(("fsdp", "heads"), None),
        P(("fsdp", "heads"), None),
        P(("fsdp", "heads")),
        P(("fsdp", "heads")),
        P("fsdp", "heads"),
        P("fsdp", "heads"),
        P("fsdp", "heads"),
        P("heads", "fsdp"),
        P("heads", "fsdp"),
        P("heads", "fsdp"),
        P(("fsdp", "heads")),
        P(("fsdp", "heads")),
        P(("fsdp", "heads")),
        P("fsdp", "heads"),
        P("heads", "fsdp"),
        P("heads", "fsdp"),
        P(("fsdp", "heads")),
    )
    return jax.shard_map(local, mesh=mesh, in_specs=in_specs, out_specs=out_specs, check_vma=False)
```

```python
import functools

import jax
import jax.numpy as jnp
from jax import lax
from jax.experimental import pallas as pl
from jax.experimental.pallas import tpu as pltpu
from jax.sharding import PartitionSpec as P

HD = 64
PAIR = 2 * HD
EPSILON = 1e-05
GELU_SCALE = 0.7978845608028654
MASKED = -1e30
F32 = jnp.float32
BF = jnp.bfloat16
NN = (((1,), (0,)), ((), ()))
NT = (((1,), (1,)), ((), ()))
TN = (((0,), (0,)), ((), ()))


def dot(left, right, dims=NN):
    return lax.dot_general(left, right, dims, preferred_element_type=F32)


def starts_of(ends_ref, position):
    start = jnp.zeros_like(position)
    for slot in range(ends_ref.shape[0]):
        start = jnp.where(position >= ends_ref[slot], ends_ref[slot], start)
    return start


def place(block, step, shift, rows):
    return pl.ds(pl.multiple_of(lax.rem(block * step + shift, rows), step), step)


def attend_kernel(rows, step, shift_ref, ends_ref, qkv_ref, mixed_ref, turned_ref, log_ref, keys, values, bias):
    shift = shift_ref[0]

    @pl.when(pl.program_id(0) == 0)
    def _():
        for i in range(rows // step):
            wide = (i + 1) * step
            row = lax.broadcasted_iota(jnp.int32, (step, 1), 0) + i * step
            column = lax.broadcasted_iota(jnp.int32, (step, wide), 1)
            seen = (column >= starts_of(ends_ref, row)) & (column <= row)
            bias[i * step : wide, :wide] = jnp.where(seen, 0.0, MASKED)

    for b in range(rows // step):
        keys[b * step : (b + 1) * step, :] = qkv_ref[place(b, step, shift, rows), PAIR : 2 * PAIR]
        values[b * step : (b + 1) * step, :] = qkv_ref[place(b, step, shift, rows), 2 * PAIR :]
    lane = lax.broadcasted_iota(jnp.int32, (step, PAIR), 1)
    second = lane >= HD
    for i in range(rows // step):
        wide = (i + 1) * step
        query = qkv_ref[place(i, step, shift, rows), :PAIR] * jnp.asarray(HD**-0.5, BF)
        mixed, logs = [], []
        for h in range(2):
            own = jnp.where(second == (h == 1), query, jnp.zeros_like(query))
            scores = dot(own, keys[:wide, :], NT) + bias[i * step : wide, :wide]
            top = jnp.max(scores, axis=1, keepdims=True)
            weights = jnp.exp(scores - top)
            total = jnp.sum(weights, axis=1, keepdims=True)
            mixed.append(dot(weights.astype(BF), values[:wide, :]) * (1.0 / total))
            logs.append(top + jnp.log(total))
        mixed = jnp.where(second, mixed[1], mixed[0]).astype(BF)
        mixed_ref[place(i, step, shift, rows), :] = mixed
        turned_ref[place(i, step, shift + rows // 2, rows), :] = mixed
        log_ref[0, :, i * step : wide] = jnp.transpose(jnp.where(lane >= 4, logs[1], logs[0]))[:8]


def attend_back_kernel(
    rows, step, shift_ref, ends_ref, qkv_ref, grad_ref, log_ref, out_ref, keys, values, bias, key_sum, value_sum
):
    shift = shift_ref[0]

    @pl.when(pl.program_id(0) == 0)
    def _():
        for i in range(rows // step):
            wide = (i + 1) * step
            row = lax.broadcasted_iota(jnp.int32, (1, step), 1) + i * step
            column = lax.broadcasted_iota(jnp.int32, (wide, step), 0)
            seen = (column >= starts_of(ends_ref, row)) & (column <= row)
            bias[:wide, i * step : wide] = jnp.where(seen, 0.0, MASKED)

    for b in range(rows // step):
        keys[b * step : (b + 1) * step, :] = qkv_ref[place(b, step, shift, rows), PAIR : 2 * PAIR]
        values[b * step : (b + 1) * step, :] = qkv_ref[place(b, step, shift, rows), 2 * PAIR :]
    second = lax.broadcasted_iota(jnp.int32, (step, PAIR), 1) >= HD
    for i in reversed(range(rows // step)):
        low, wide = i * step, (i + 1) * step
        query = qkv_ref[place(i, step, shift, rows), :PAIR] * jnp.asarray(HD**-0.5, BF)
        grad = grad_ref[place(i, step, shift, rows), :]
        to_query, to_key, to_value = [], [], []
        for h in range(2):
            own_query = jnp.where(second == (h == 1), query, jnp.zeros_like(query))
            own_grad = jnp.where(second == (h == 1), grad, jnp.zeros_like(grad))
            scores = dot(keys[:wide, :], own_query, NT) + bias[:wide, low:wide]
            probs = jnp.exp(scores - log_ref[0, 4 * h : 4 * h + 1, low:wide])
            grad_probs = dot(values[:wide, :], own_grad, NT)
            spread = jnp.sum(probs * grad_probs, axis=0, keepdims=True)
            grad_scores = (probs * (grad_probs - spread)).astype(BF)
            to_value.append(dot(probs.astype(BF), own_grad))
            to_key.append(dot(grad_scores, own_query))
            to_query.append(dot(grad_scores, keys[:wide, :], TN))
        grad_query = jnp.where(second, to_query[1], to_query[0]) * (HD**-0.5)
        grad_key = to_key[0] + to_key[1]
        grad_value = to_value[0] + to_value[1]
        if wide < rows:
            grad_key = grad_key + key_sum[:wide, :]
            grad_value = grad_value + value_sum[:wide, :]
        out_ref[place(i, step, shift, rows), :PAIR] = grad_query.astype(BF)
        out_ref[place(i, step, shift, rows), PAIR : 2 * PAIR] = grad_key[low:, :].astype(BF)
        out_ref[place(i, step, shift, rows), 2 * PAIR :] = grad_value[low:, :].astype(BF)
        if low > 0:
            key_sum[:low, :] = grad_key[:low, :]
            value_sum[:low, :] = grad_value[:low, :]


def attend(shift, ends, qkv, pairs):
    rows = qkv.shape[0]
    step = min(256, rows)
    work = 2 * pairs * rows * rows
    return pl.pallas_call(
        functools.partial(attend_kernel, rows, step),
        grid_spec=pltpu.PrefetchScalarGridSpec(
            num_scalar_prefetch=2,
            grid=(pairs,),
            in_specs=[pl.BlockSpec((rows, 3 * PAIR), lambda p, *_: (0, p))],
            out_specs=[
                pl.BlockSpec((rows, PAIR), lambda p, *_: (0, p)),
                pl.BlockSpec((rows, PAIR), lambda p, *_: (0, p)),
                pl.BlockSpec((1, 8, rows), lambda p, *_: (p, 0, 0)),
            ],
            scratch_shapes=[
                pltpu.VMEM((rows, PAIR), BF),
                pltpu.VMEM((rows, PAIR), BF),
                pltpu.VMEM((rows, rows), F32),
            ],
        ),
        out_shape=[
            jax.ShapeDtypeStruct((rows, PAIR * pairs), BF),
            jax.ShapeDtypeStruct((rows, PAIR * pairs), BF),
            jax.ShapeDtypeStruct((pairs, 8, rows), F32),
        ],
        compiler_params=pltpu.CompilerParams(vmem_limit_bytes=40 << 20),
        cost_estimate=pl.CostEstimate(
            flops=work * 128, bytes_accessed=rows * PAIR * pairs * 8, transcendentals=0
        ),
        name="attend",
    )(shift, ends, qkv)


def attend_back(shift, ends, qkv, grad_mixed, logs, first, pairs):
    rows = qkv.shape[0]
    step = min(256, rows)
    work = 2 * pairs * rows * rows
    return pl.pallas_call(
        functools.partial(attend_back_kernel, rows, step),
        grid_spec=pltpu.PrefetchScalarGridSpec(
            num_scalar_prefetch=2,
            grid=(pairs,),
            in_specs=[
                pl.BlockSpec((rows, 3 * PAIR), lambda p, *_: (0, p)),
                pl.BlockSpec((rows, PAIR), lambda p, *_: (0, p + first)),
                pl.BlockSpec((1, 8, rows), lambda p, *_: (p, 0, 0)),
            ],
            out_specs=pl.BlockSpec((rows, 3 * PAIR), lambda p, *_: (0, p)),
            scratch_shapes=[
                pltpu.VMEM((rows, PAIR), BF),
                pltpu.VMEM((rows, PAIR), BF),
                pltpu.VMEM((rows, rows), F32),
                pltpu.VMEM((rows, PAIR), F32),
                pltpu.VMEM((rows, PAIR), F32),
            ],
        ),
        out_shape=jax.ShapeDtypeStruct((rows, 3 * PAIR * pairs), BF),
        compiler_params=pltpu.CompilerParams(vmem_limit_bytes=40 << 20),
        cost_estimate=pl.CostEstimate(
            flops=work * 256, bytes_accessed=rows * PAIR * pairs * 14, transcendentals=0
        ),
        name="attend_back",
    )(shift, ends, qkv, grad_mixed, logs)


def norm_kernel(parts, gain_ref, shift_ref, *refs):
    part = pl.program_id(0) // (pl.num_programs(0) // parts)
    for i in range(parts):

        @pl.when(part == i)
        def _(i=i):
            rows = refs[i][...].astype(F32)
            centered = rows - jnp.mean(rows, axis=-1, keepdims=True)
            scale = lax.rsqrt(jnp.mean(centered * centered, axis=-1, keepdims=True) + EPSILON)
            refs[parts][...] = (centered * scale * gain_ref[...] + shift_ref[...]).astype(BF)


def norm_all(arrays, gain, shift):
    share, width = arrays[0].shape
    step = min(256, share)
    per, parts = share // step, len(arrays)
    line = pl.BlockSpec((1, width), lambda i: (0, 0))
    return pl.pallas_call(
        functools.partial(norm_kernel, parts),
        grid=(per * parts,),
        in_specs=[line, line]
        + [
            pl.BlockSpec((step, width), lambda i, k=k: (jnp.clip(i - k * per, 0, per - 1), 0))
            for k in range(parts)
        ],
        out_specs=pl.BlockSpec((step, width), lambda i: (i, 0)),
        out_shape=jax.ShapeDtypeStruct((share * parts, width), BF),
        compiler_params=pltpu.CompilerParams(vmem_limit_bytes=32 << 20),
        cost_estimate=pl.CostEstimate(flops=0, bytes_accessed=share * parts * width * 4, transcendentals=0),
        name="norm_all",
    )(gain, shift, *arrays)


def spread_kernel(depth, units, each, pairs, flat_ref, wide_ref, up_ref, qkv_ref):
    devices = flat_ref.shape[0]

    def laid(row, lane, size):
        total = devices * size
        source = flat_ref[:, row, :]
        at = lax.broadcasted_iota(jnp.int32, (128, total), 1) & (size - 1)
        pick = (lax.broadcasted_iota(jnp.int32, (128, total), 0) == at + lane).astype(BF)
        owner = lax.broadcasted_iota(jnp.int32, (devices, total), 1) // size
        mine = owner == lax.broadcasted_iota(jnp.int32, (devices, total), 0)
        return jnp.sum(jnp.where(mine, dot(source, pick), 0.0), axis=0, keepdims=True)

    for i in range(6):
        wide_ref[i : i + 1, :] = laid(i, 0, depth)
    for h in range(2 * pairs):
        up_ref[:, h * devices * units : (h + 1) * devices * units] = laid(8 + h, 0, units)
    for p in range(pairs):
        for k in range(3):
            column = (3 * p + k) * PAIR
            if k == 1:
                qkv_ref[:, column : column + PAIR] = jnp.zeros((1, PAIR), F32)
                continue
            lane = units + (each if k == 2 else 0)
            halves = [laid(8 + 2 * p + h, lane, each) for h in range(2)]
            qkv_ref[:, column : column + PAIR] = jnp.concatenate(halves, 1)


def spread(flat, depth, units, each, pairs):
    devices = flat.shape[0]
    shapes = [(6, devices * depth), (1, 2 * pairs * devices * units), (1, 3 * PAIR * pairs)]
    return pl.pallas_call(
        functools.partial(spread_kernel, depth, units, each, pairs),
        out_shape=[jax.ShapeDtypeStruct(shape, F32) for shape in shapes],
        compiler_params=pltpu.CompilerParams(vmem_limit_bytes=32 << 20),
        name="spread",
    )(flat)


def feed_kernel(normed_ref, grad_ref, up_ref, down_ref, bias_ref, hidden_ref, out_ref, sum_ref):
    step = min(256, normed_ref.shape[0])
    total = None
    for i in range(normed_ref.shape[0] // step):
        rows = slice(i * step, (i + 1) * step)
        pre = dot(normed_ref[rows, :], up_ref[...]) + bias_ref[...]
        squared = pre * pre
        bend = 0.5 + 0.5 * jnp.tanh(pre * (GELU_SCALE + (GELU_SCALE * 0.044715) * squared))
        hidden = pre * bend
        hidden_ref[rows, :] = hidden.astype(BF)
        slope = bend + hidden * (1.0 - bend) * (2 * GELU_SCALE + (6 * GELU_SCALE * 0.044715) * squared)
        grad = (slope * dot(grad_ref[rows, :], down_ref[...])).astype(BF)
        out_ref[rows, :] = grad
        part = jnp.sum(grad.astype(F32), axis=0, keepdims=True)
        total = part if total is None else total + part
    sum_ref[...] = total


def feed(normed, grad_out, up_w, down_w, up_b):
    rows, width = normed.shape
    units = up_w.shape[1]
    step = min(512, units)
    whole = pl.BlockSpec((rows, width), lambda i: (0, 0))
    columns = pl.BlockSpec((width, step), lambda i: (0, i))
    line = pl.BlockSpec((1, step), lambda i: (0, i))
    out = pl.BlockSpec((rows, step), lambda i: (0, i))
    return pl.pallas_call(
        feed_kernel,
        grid=(units // step,),
        in_specs=[whole, whole, columns, columns, line],
        out_specs=[out, out, line],
        out_shape=[
            jax.ShapeDtypeStruct((rows, units), BF),
            jax.ShapeDtypeStruct((rows, units), BF),
            jax.ShapeDtypeStruct((1, units), F32),
        ],
        compiler_params=pltpu.CompilerParams(vmem_limit_bytes=44 << 20),
        cost_estimate=pl.CostEstimate(flops=rows * units * width, bytes_accessed=1 << 20, transcendentals=0),
        name="feed",
    )(normed, grad_out, up_w, down_w, up_b)


BITS = 4


def lined():
    return lax.axis_size("fsdp") == 1 << BITS


def bit_of(axis):
    return (lax.axis_index("fsdp") >> (BITS - 1 - axis)) & 1


def trade(array, axis):
    flip = 1 << (BITS - 1 - axis)
    return lax.ppermute(array, "fsdp", [(i, i ^ flip) for i in range(1 << BITS)])


def after(array, *earlier):
    earlier = tuple(e for e in earlier if e is not None)
    return lax.optimization_barrier((array,) + earlier)[0] if earlier else array


def interleave_kernel(core_ref, own_ref, other_ref, out_ref):
    core = core_ref[0]
    for i in range(own_ref.shape[0]):
        out_ref[i, core] = own_ref[i]
        out_ref[i, 1 - core] = other_ref[i]


def interleave(core, own, other):
    n, r, c = own.shape
    per = 2
    spec = pl.BlockSpec((per, r, c), lambda i, *_: (i, 0, 0))
    return pl.pallas_call(
        interleave_kernel,
        grid_spec=pltpu.PrefetchScalarGridSpec(
            num_scalar_prefetch=1,
            grid=(n // per,),
            in_specs=[spec, spec],
            out_specs=pl.BlockSpec((per, 2, r, c), lambda i, *_: (i, 0, 0, 0)),
        ),
        out_shape=jax.ShapeDtypeStruct((n, 2, r, c), own.dtype),
        compiler_params=pltpu.CompilerParams(vmem_limit_bytes=32 << 20),
        cost_estimate=pl.CostEstimate(flops=0, bytes_accessed=own.size * 8, transcendentals=0),
        name="interleave",
    )(core.reshape(1).astype(jnp.int32), own, other)


def placed(parts):
    array, other, axis, at = parts
    if other is None:
        return array
    return jnp.where(bit_of(axis) == 1, jnp.stack([other, array], at), jnp.stack([array, other], at))


class Gather:
    def __init__(self, shard, order=(0, 1, 2)):
        self.parts, self.order, self.passed, self.width = (shard, None, 0, 0), list(order), [], shard.shape[1]
        self.payload = None

    def take(self, earlier):
        array, other, axis, at = self.parts
        if other is None:
            return after(array, *earlier)
        array, other = after((array, other), *earlier)
        return placed((array, other, axis, at))

    def step(self, *earlier):
        block = self.take(earlier)
        if not lined():
            if not self.passed:
                block = lax.all_gather(block, "fsdp", axis=0, tiled=True)
                self.parts, self.passed = (block, None, 0, 0), [0]
            return block
        axis = self.order.pop(0)
        at = sum(p < axis for p in self.passed)
        self.passed.append(axis)
        self.payload = block
        other = trade(block, axis)
        self.parts = (block, other, axis, at)
        return other

    def end(self, *earlier):
        if not lined():
            return self.step(*earlier)
        while self.order:
            self.step(*earlier)
        block = self.take(earlier).reshape(8, -1, self.width)
        other = trade(block, 3)
        if block.shape[1] * self.width < 1 << 15:
            whole = placed((block, other, 3, 1))
        else:
            whole = interleave(bit_of(3), block, other)
        return whole.reshape(-1, self.width)


def at_index(array, index, axis):
    return lax.dynamic_index_in_dim(array, index, axis, keepdims=False)


class Halver:
    def __init__(self, parts, axes, order, last):
        self.own, self.got, self.left, self.order, self.last = parts, None, list(axes), list(order), last
        self.payload, self.result = None, None

    def take(self, earlier):
        if self.got is None:
            return after(self.own, *earlier)
        own, got = after((self.own, self.got), *earlier)
        total = own.astype(F32) + got.astype(F32)
        return total if not self.order and self.last else total.astype(own.dtype)

    def step(self, *earlier):
        if not self.order:
            return None
        axis = self.order[0]
        at = self.left.index(axis)
        parts = self.take(earlier)
        self.order.pop(0)
        self.left.remove(axis)
        mine = bit_of(axis)
        self.payload = at_index(parts, 1 - mine, at)
        self.got = trade(self.payload, axis)
        self.own = at_index(parts, mine, at)
        return self.got


class Exchange:
    def __init__(self, whole):
        self.rows, self.got, self.payload, self.result = whole.shape[0], None, None, None
        if lined():
            self.own, self.order = whole.reshape((4, 4, -1) + whole.shape[1:]), [1, 0]
        else:
            self.own, self.order = lax.psum_scatter(whole, "fsdp", scatter_dimension=0, tiled=True), []

    def take(self, earlier):
        own, got = after((self.own, tuple(self.got or ())), *earlier)
        return own + sum(got) if got else own

    def step(self, *earlier):
        parts = self.take(earlier)
        at = self.order.pop(0)
        mine = (lax.axis_index("fsdp") >> (0 if at else 2)) & 3
        self.own = at_index(parts, mine, at)
        self.got = []
        for flip in range(1, 4):
            pairs = [(i, i ^ (flip << (0 if at else 2))) for i in range(16)]
            self.got.append(lax.ppermute(at_index(parts, mine ^ flip, at), "fsdp", pairs))
        return self.got[-1]


def columns_of(array, index):
    width = array.shape[1] // 2
    return lax.dynamic_slice_in_dim(array, index * width, width, 1)


class Weigh(Halver):
    def __init__(self, left, right, order=(2, 1, 0)):
        if not lined():
            total = lax.psum_scatter(dot(left, right, TN).astype(BF), "fsdp", scatter_dimension=0, tiled=True)
            super().__init__(total.astype(F32), (), (), True)
            return
        core = bit_of(3)
        got = trade(dot(left, columns_of(right, 1 - core), TN).astype(BF), 3)
        total = (dot(left, columns_of(right, core), TN) + got.astype(F32)).astype(BF)
        super().__init__(total.reshape(2, 2, 2, -1, total.shape[1]), (0, 1, 2), order, True)

    def end(self, *earlier):
        total = self.take(earlier)
        if not lined():
            return total
        core = bit_of(3)
        total = total.reshape(2, -1, total.shape[1])
        got = trade(at_index(total, 1 - core, 0).astype(BF), 3)
        return at_index(total, core, 0), got


def joined(result):
    if not lined():
        return result
    own, got = result[0], result[1].astype(F32)
    return jnp.where(bit_of(3) == 1, jnp.concatenate([got, own], 1), jnp.concatenate([own, got], 1))


def unpack_kernel(count, core_ref, *refs):
    core = core_ref[0]
    for g in range(count):
        for half, part in enumerate(refs[2 * g : 2 * g + 2]):
            pair = 2 * g + (core if half == 0 else 1 - core)
            columns = pl.ds(pl.multiple_of(pair * PAIR, PAIR), PAIR)
            for k in range(3):
                refs[2 * count + 2 + k][:, columns] = part[:, k * PAIR : (k + 1) * PAIR].astype(F32)
    width = refs[2 * count].shape[1]
    for half in range(2):
        place_at = core if half == 0 else 1 - core
        columns = pl.ds(pl.multiple_of(place_at * width, 128), width)
        refs[2 * count + 5][:, columns] = refs[2 * count + half][...].astype(F32)


def unpack(core, groups, up):
    rows, width = groups[0][0].shape[0], len(groups) * 2 * PAIR
    shapes = [(rows, width)] * 3 + [(rows, 2 * up[0].shape[1])]
    return pl.pallas_call(
        functools.partial(unpack_kernel, len(groups)),
        in_specs=[pl.BlockSpec(memory_space=pltpu.SMEM)]
        + [pl.BlockSpec(memory_space=pltpu.VMEM)] * (2 * len(groups) + 2),
        out_specs=[pl.BlockSpec(memory_space=pltpu.VMEM)] * 4,
        out_shape=[jax.ShapeDtypeStruct(shape, F32) for shape in shapes],
        compiler_params=pltpu.CompilerParams(vmem_limit_bytes=32 << 20),
        name="unpack",
    )(core.reshape(1).astype(jnp.int32), *[half for group in groups for half in group], *up)


def pack_kernel(counts, *refs):
    weights, outs, pair = refs[:3], refs[3:], 0
    for out, count in zip(outs, counts):
        for p in range(count):
            for k in range(3):
                column = (3 * p + k) * PAIR
                out[:, column : column + PAIR] = weights[k][:, pair * PAIR : (pair + 1) * PAIR]
            pair += 1


def pack(weights, counts):
    rows = weights[0].shape[0]
    return pl.pallas_call(
        functools.partial(pack_kernel, counts),
        out_shape=[jax.ShapeDtypeStruct((rows, 3 * PAIR * count), BF) for count in counts],
        compiler_params=pltpu.CompilerParams(vmem_limit_bytes=32 << 20),
        name="pack",
    )(*weights)


def lines_kernel(*refs):
    lines, out, rows = refs[:-2], refs[-2], refs[-1]
    rows[...] = jnp.zeros_like(rows)
    for i, line in enumerate(lines[:6]):
        rows[i : i + 1, : line.shape[1]] = line[...].astype(F32)
    lane = 0
    for line in lines[6:]:
        rows[8 : 8 + line.shape[0], lane : lane + line.shape[1]] = line[...].astype(F32)
        lane += line.shape[1]
    out[...] = rows[...].astype(BF)


def pack_lines(lines):
    return pl.pallas_call(
        lines_kernel,
        out_shape=jax.ShapeDtypeStruct((16, 128), BF),
        scratch_shapes=[pltpu.VMEM((16, 128), F32)],
        compiler_params=pltpu.CompilerParams(vmem_limit_bytes=32 << 20),
        name="pack_lines",
    )(*lines)


def paired():
    return lax.axis_size("heads") == 2


def swap(array):
    return lax.ppermute(array, "heads", [(0, 1), (1, 0)])


def heads_rows(share):
    if not paired():
        return lax.all_gather(share, "heads", axis=0, tiled=True)
    return jnp.concatenate([share, swap(share)], 0)


def heads_columns(share):
    if not paired():
        return lax.all_gather(share, "heads", axis=1, tiled=True)
    return jnp.concatenate([share, swap(share)], 1)


def heads_partials(left, right, dims):
    if not paired():
        return [dot(left, right, dims)]
    share = left.shape[0] // 2
    theirs = dot(left[share:], right, dims)
    return [dot(left[:share], right, dims), theirs]


def heads_send(partials, *earlier):
    if not paired():
        partial = after(partials[0].astype(BF), *earlier)
        return lax.psum_scatter(partial, "heads", scatter_dimension=0, tiled=True)
    return swap(after(partials[1].astype(BF), *earlier))


def heads_sum(partials, got):
    return partials[0].astype(F32) + got.astype(F32) if paired() else got.astype(F32)


def heads_exchange(columns):
    if not paired():
        return lax.all_to_all(columns, "heads", 1, 0, tiled=True)
    width = columns.shape[1] // 2
    return jnp.concatenate([columns[:, :width], swap(columns[:, width:])], 0)


def norm_parts(rows):
    mean = jnp.mean(rows, axis=-1, keepdims=True)
    centered = rows - mean
    scale = lax.rsqrt(jnp.mean(centered * centered, axis=-1, keepdims=True) + EPSILON)
    return centered * scale, scale


def norm_back(grad, hat, scale, gain):
    e = grad * gain
    return scale * (e - jnp.mean(e, -1, keepdims=True) - hat * jnp.mean(e * hat, -1, keepdims=True))


def local(
    tokens,
    ln1_gain,
    ln1_bias,
    w_query,
    w_key,
    w_value,
    bias_query,
    bias_value,
    w_out,
    bias_out,
    ln2_gain,
    ln2_bias,
    w_up,
    bias_up,
    w_down,
    bias_down,
    cotangent,
    seq_lengths,
):
    share = tokens.shape[0]
    rows = share * lax.axis_size("heads")
    depth = ln1_gain.shape[0]
    width = w_query.shape[1]
    pairs = width // PAIR
    groups = [(0, pairs)] if pairs < 2 else [(0, pairs // 2), (pairs // 2, pairs - pairs // 2)]
    here = lax.axis_index("heads")
    shift = (here * share if paired() else jnp.zeros((), jnp.int32)).astype(jnp.int32).reshape(1)
    ends = jnp.cumsum(seq_lengths[0]).astype(jnp.int32)
    live = (here * share + jnp.arange(share, dtype=jnp.int32) < ends[-1]).astype(F32)

    blocks, heads, units, each = lax.axis_size("fsdp"), bias_query.shape[0], bias_up.shape[1], bias_query.shape[1]
    shards = [Gather(a) for a in pack((w_query, w_key, w_value), [count for _, count in groups])]
    vectors = (ln1_gain, ln1_bias, bias_out, ln2_gain, ln2_bias, bias_down)
    lines = [v.reshape(1, depth) for v in after(vectors, shards[0].parts[0])] + [bias_up, bias_query, bias_value]
    small = Gather(pack_lines(lines))
    tokens_other = swap(tokens) if paired() else None
    out_shard = Gather(heads_columns(w_out.T))
    up_shard = Gather(w_up)
    down_shard = Gather(w_down.T)
    full_width = out_shard.width
    rounds = lined() and len(shards) == 2
    if rounds:
        ended = [shards[0].step(), small.step()]
        ended = [shards[0].step(*ended), small.step(*ended), shards[1].step(*ended)]
        ended += [tokens_other]
        ended = [shards[0].step(*ended), small.step(*ended), shards[1].step(*ended), out_shard.step(*ended)]
        qkv_w = [shards[0].end(*ended)]
        flat = small.end(*ended)
        ended = [shards[1].step(*ended), out_shard.step(*ended), up_shard.step(*ended)]
    else:
        qkv_w = [shard.end() for shard in shards]
        flat = small.end()
    vectors, up_b, qkv_b = spread(flat.reshape(blocks, -1, 128), depth, units, each, pairs)
    gain_one, shift_one, out_b, gain_two, shift_two, down_b = [vectors[i : i + 1] for i in range(6)]

    grad_out = (cotangent.astype(F32) * live[:, None]).astype(BF)
    grad_out_full = heads_rows(after(grad_out, tokens_other))
    if paired():
        rows_full = jnp.concatenate([tokens, tokens_other], 0).astype(F32)
    else:
        rows_full = lax.all_gather(tokens, "heads", axis=0, tiled=True).astype(F32)
    own_rows = lambda array: lax.dynamic_slice_in_dim(array, 0 if paired() else here * share, share, 0)
    normed_one = norm_all([tokens, tokens_other] if paired() else [rows_full], gain_one, shift_one)
    mixed, others, logs, qkv = [], [], [], []
    for g, (first, count) in enumerate(groups):
        bias = qkv_b[:, first * 3 * PAIR : (first + count) * 3 * PAIR]
        projected = (dot(normed_one, qkv_w[g]) + bias).astype(BF)
        if rounds and g == 0:
            projected = after(projected, *ended)
            qkv_w.append(shards[1].end(projected))
            out_shard.step(projected)
            up_shard.step(projected)
            down_shard.step(projected)
            projected = after(projected, out_shard.payload, up_shard.payload)
        elif rounds:
            up_shard.step(mixed[0])
            down_shard.step(mixed[0])
            projected = after(projected, up_shard.payload, down_shard.payload)
        qkv.append(projected)
        part, turned, log = attend(shift, ends, projected, count)
        mixed.append(part)
        logs.append(log)
        if paired():
            others.append(swap(after(turned, others[-1] if others else grad_out_full)))
    down_shard.step(mixed[-1])
    out_w = out_shard.end(mixed[-1])
    up_w = up_shard.end(out_w)
    down_w = down_shard.end(out_w)
    mixed = jnp.concatenate(mixed, 1)
    if paired():
        mixed_full = jnp.concatenate([mixed] + others, 1)
    else:
        mixed_full = lax.all_gather(mixed, "heads", axis=1, tiled=True)
    mid = rows_full + dot(mixed_full, out_w, NT) + out_b
    hat_two, scale_two = norm_parts(mid)
    normed_two = (hat_two * gain_two + shift_two).astype(BF)

    hidden, grad_pre, grad_up_b = feed(normed_two, grad_out_full, up_w, down_w, up_b)
    partials_two = heads_partials(grad_pre, up_w, NT)
    got_two = heads_send(partials_two)
    down_sum = Weigh(grad_out_full, hidden)
    up_sum = Weigh(normed_two, grad_pre, (1, 0, 2))
    down_sum.step()
    up_sum.step()
    grad_mid = grad_out.astype(F32) + norm_back(
        heads_sum(partials_two, after(got_two, up_sum.payload, down_sum.payload)), own_rows(hat_two), own_rows(scale_two), gain_two
    )
    grad_branch = grad_mid.astype(BF)
    mixing = heads_exchange(dot(grad_branch, out_w).astype(BF))
    out_sum = Weigh(grad_branch, own_rows(mixed_full))
    partials = lax.optimization_barrier(heads_partials(hidden, down_w, NT))
    hats = jnp.split(hat_two, len(partials_two))
    grad_gain_two = sum(jnp.sum(p * h, 0) for p, h in zip(partials_two, hats))
    grad_shift_two = sum(jnp.sum(p, 0) for p in partials_two)

    out_sum.step()
    grad_mixed = after(mixing, out_sum.own, out_sum.payload, grad_gain_two, grad_shift_two)
    got_forward = heads_send(partials, mixing)
    grad_qkv, sums = [], []
    for g, ((first, count), log, part) in enumerate(zip(groups, logs, qkv)):
        if g > 0:
            sums.append(Weigh(normed_one, grad_qkv[-1]))
            lines = [sums[-1], up_sum, down_sum, out_sum]
            for line in lines:
                line.step(grad_qkv[-1])
            grad_mixed = after(grad_mixed, grad_qkv[-1], *[line.payload for line in lines])
        part = attend_back(shift, ends, part, grad_mixed, log, first, count)
        grad_qkv.append(part)
    partials_one = heads_partials(jnp.concatenate(grad_qkv, 1), jnp.concatenate(qkv_w, 1), NT)
    got_one = heads_send(partials_one, got_forward)
    partials_one = lax.optimization_barrier(partials_one)
    sums.append(Weigh(normed_one, after(grad_qkv[-1], partials_one[-1])))
    hat_one, scale_one = norm_parts(rows_full)
    hats = jnp.split(hat_one, len(partials_one))
    grad_gain_one = sum(jnp.sum(p * h, 0) for p, h in zip(partials_one, hats))
    grad_shift_one = sum(jnp.sum(p, 0) for p in partials_one)
    grad_qkv_b = jnp.concatenate([jnp.sum(part, axis=0, dtype=F32) for part in grad_qkv]).reshape(pairs, 3, PAIR)

    wide = [
        v.reshape(blocks, depth)
        for v in (
            grad_gain_one,
            grad_shift_one,
            jnp.sum(grad_branch, axis=0, dtype=F32),
            grad_gain_two,
            grad_shift_two,
            jnp.sum(grad_out, axis=0, dtype=F32),
        )
    ]
    narrow = [
        jnp.swapaxes(v.reshape(heads, blocks, -1), 0, 1).reshape(blocks, -1)
        for v in (grad_up_b, grad_qkv_b[:, 0], grad_qkv_b[:, 2])
    ]
    packed = jnp.concatenate(wide + narrow, 1)
    used = packed.shape[1]
    padded = -(-used // 1024) * 1024
    packed = jnp.pad(packed, ((0, 0), (0, padded - used))).reshape(blocks * (padded // 128), 128)
    packed = Exchange(packed)
    lines = sums[::-1] + [up_sum, down_sum, out_sum]
    ended, count = [sums[-1].own], 0
    while lines:
        begun = []
        for line in lines:
            if line.order:
                begun.append(line.step(*ended))
            else:
                line.result = line.end(*ended)
        if count > 0 and packed.order:
            begun.append(packed.step(*ended))
        lines = [line for line in lines if line.result is None]
        ended, count = begun, count + 1
        if count == 2:
            got_one = after(got_one, *ended)
            ended = [got_one]
    while packed.order:
        packed.step()
    if lined() and width == 2 * PAIR * len(groups):
        *grad_qkv_w, grad_up_w = unpack(bit_of(3), [line.result for line in sums], up_sum.result)
    else:
        grad_up_w = joined(up_sum.result)
        grad_qkv_w = jnp.concatenate([joined(line.result) for line in sums], 1).reshape(depth, pairs, 3, PAIR)
        grad_qkv_w = [grad_qkv_w[:, :, k].reshape(depth, width) for k in range(3)]
    grad_out_w = joined(out_sum.result)
    grad_down_w = joined(down_sum.result)
    if paired():
        width_out = grad_out_w.shape[1] // 2
        grad_out_w = grad_out_w[:, :width_out] + swap(grad_out_w[:, width_out:])
    else:
        grad_out_w = lax.psum_scatter(grad_out_w, "heads", scatter_dimension=1, tiled=True)
    output = (own_rows(mid) + heads_sum(partials, got_forward) + down_b).astype(BF)
    grad_normed_one = heads_sum(partials_one, got_one)
    grad_input = grad_mid + norm_back(grad_normed_one, own_rows(hat_one), own_rows(scale_one), gain_one)
    packed = packed.take(()).reshape(-1)
    over_heads = packed[: 6 * depth].reshape(6, -1, depth // lax.axis_size("heads"))
    if paired():
        theirs = lax.dynamic_index_in_dim(over_heads, 1 - here, 1, keepdims=False)
        vector = lax.dynamic_index_in_dim(over_heads, here, 1, keepdims=False) + swap(theirs)
    else:
        vector = lax.psum(over_heads, "heads")
        vector = lax.dynamic_index_in_dim(vector, here, 1, keepdims=False)
    at = 6 * depth
    flat_grads = []
    for shard in (bias_up, bias_query, bias_value):
        flat_grads.append(packed[at : at + shard.size].reshape(shard.shape))
        at += shard.size
    return (
        output,
        grad_input,
        vector[0],
        vector[1],
        *grad_qkv_w,
        flat_grads[1],
        flat_grads[2],
        grad_out_w.T,
        vector[2],
        vector[3],
        vector[4],
        grad_up_w,
        flat_grads[0],
        grad_down_w.T,
        vector[5],
    )


def solution(mesh):
    in_specs = (
        P(("fsdp", "heads"), None),
        P("fsdp"),
        P("fsdp"),
        P("fsdp", "heads"),
        P("fsdp", "heads"),
        P("fsdp", "heads"),
        P("heads", "fsdp"),
        P("heads", "fsdp"),
        P("heads", "fsdp"),
        P("fsdp"),
        P("fsdp"),
        P("fsdp"),
        P("fsdp", "heads"),
        P("heads", "fsdp"),
        P("heads", "fsdp"),
        P("fsdp"),
        P(("fsdp", "heads"), None),
        P("fsdp", None),
    )
    out_specs = (
        P(("fsdp", "heads"), None),
        P(("fsdp", "heads"), None),
        P(("fsdp", "heads")),
        P(("fsdp", "heads")),
        P("fsdp", "heads"),
        P("fsdp", "heads"),
        P("fsdp", "heads"),
        P("heads", "fsdp"),
        P("heads", "fsdp"),
        P("heads", "fsdp"),
        P(("fsdp", "heads")),
        P(("fsdp", "heads")),
        P(("fsdp", "heads")),
        P("fsdp", "heads"),
        P("heads", "fsdp"),
        P("heads", "fsdp"),
        P(("fsdp", "heads")),
    )
    return jax.shard_map(local, mesh=mesh, in_specs=in_specs, out_specs=out_specs, check_vma=False)
```
